256 devices in a mesh: cols: 64 (over x_hi, z, y), rows: 4 (over x_lo, core).
Axes of the slice: x: 4 (x_hi: 2, x_lo: 2; x = x_hi * 2 + x_lo), y: 4, z: 8, core: 2. Of those that a mesh axis runs over, the one named last changes fastest.
Arguments:
- image: bfloat16 [64, 1024, 512], P('rows', 'cols'), may hold values from -6 to 6
- w_qkv: bfloat16 [512, 1536], replicated, may hold values from -0.25 to 0.25
- b_qkv: float32 [1536], replicated, may hold values from -3 to 3
- logit_scale: float32 [16], replicated, may hold values from 0.7 to 3
- bias_table: float32 [16, 961], replicated, may hold values from -5 to 5
- w_proj: bfloat16 [512, 512], replicated, may hold values from -0.25 to 0.25
- b_proj: float32 [512], replicated, may hold values from -3 to 3
- gain_attn: float32 [512], replicated, may hold values from 0.25 to 1.75
- shift_attn: float32 [512], replicated, may hold values from -3 to 3
- w_merge: bfloat16 [2048, 1024], replicated, may hold values from -0.125 to 0.125
- gain_merge: float32 [1024], replicated, may hold values from 0.25 to 1.75
- shift_merge: float32 [1024], replicated, may hold values from -3 to 3
- grad_out: bfloat16 [32, 512, 1024], P('rows', 'cols'), may hold values from -6 to 6
Outputs:
- merged: bfloat16 [32, 512, 1024], P('rows', 'cols')
- grad_image: bfloat16 [64, 1024, 512], P('rows', 'cols')
- grad_qkv: float32 [786432], P(('cols', 'rows'))
- grad_proj: float32 [262144], P(('cols', 'rows'))
- grad_merge: float32 [2097152], P(('cols', 'rows'))
The draws below stay inside these ranges and needn't reach their ends.
All inputs are finite; a program needn't handle non-finite values.
Results may differ from the reference program's by a relative error of at most 0.013.
Values may be sent and summed in bfloat16 or wider, within the bound.
A program may use at most 128 MiB of HBM per device.

```python
import math
import jax
import jax.numpy as jnp
from jax import lax

CH = 512
HEADS = 16
WIN = 16
BUCKETS = 961
GRID_ROWS = 64
GRID_COLS = 1024
MERGED = 16384


def block_levels(rng, dims, cuts, low, high):
    loudness = 1.0
    for dim, blocks in cuts:
        draws = jax.random.uniform(jax.random.fold_in(jax.random.fold_in(rng, 6), dim), (blocks,), jnp.float32, low / len(cuts), high / len(cuts))
        loudness = loudness * jnp.repeat(jnp.exp(draws), dims[dim] // blocks).reshape((-1,) + (1,) * (len(dims) - 1 - dim))
    return loudness


def noise(rng, extent, deviation, most, shards=(), kind=jnp.bfloat16):
    array = deviation * jax.random.normal(rng, extent, jnp.float32)
    if shards:
        array = array * block_levels(rng, extent, shards, -0.22, 0.18)
    return jnp.clip(array, -most, most).astype(kind)


def setup_inputs(seed: int = 0) -> dict:
    seeds = jax.random.split(jax.random.key(seed), 14)
    image = noise(seeds[0], (GRID_ROWS, GRID_COLS, CH), 1.0, 6.0, ((0, 4), (1, 64)))
    w_qkv = noise(seeds[1], (CH, 3 * CH), CH ** -0.5, 0.25)
    b_qkv = noise(seeds[2], (3 * CH,), 0.5, 3.0, (), jnp.float32)
    logit_scale = jnp.clip(jax.random.uniform(seeds[3], (HEADS,), jnp.float32, 0.7, 3.0), 0.7, 3.0)
    bias_table = noise(seeds[4], (HEADS, BUCKETS), 1.5, 5.0, (), jnp.float32)
    w_proj = noise(seeds[5], (CH, CH), CH ** -0.5, 0.25)
    b_proj = noise(seeds[6], (CH,), 0.5, 3.0, (), jnp.float32)
    gain_attn = jnp.clip(1.0 + 0.15 * jax.random.normal(seeds[7], (CH,), jnp.float32), 0.25, 1.75)
    shift_attn = noise(seeds[8], (CH,), 0.5, 3.0, (), jnp.float32)
    w_merge = noise(seeds[9], (4 * CH, 2 * CH), (4 * CH) ** -0.5, 0.125)
    gain_merge = jnp.clip(1.0 + 0.15 * jax.random.normal(seeds[10], (2 * CH,), jnp.float32), 0.25, 1.75)
    shift_merge = noise(seeds[11], (2 * CH,), 0.5, 3.0, (), jnp.float32)
    grad_out = noise(seeds[12], (GRID_ROWS // 2, GRID_COLS // 2, 2 * CH), 1.0, 6.0, ((0, 4), (1, 64)))
    return dict(image=image, w_qkv=w_qkv, b_qkv=b_qkv, logit_scale=logit_scale, bias_table=bias_table, w_proj=w_proj, b_proj=b_proj, gain_attn=gain_attn, shift_attn=shift_attn, w_merge=w_merge, gain_merge=gain_merge, shift_merge=shift_merge, grad_out=grad_out)


EPS_NORM = 1e-05
EPS_COS = 1e-06
HIGH = lax.Precision.HIGHEST

def low_einsum(form, left, right):
    return jnp.einsum(form, left.astype(jnp.float32), right.astype(jnp.float32), precision=HIGH)

def contract_rows(left, right):
    return lax.dot_general(left, right, (((0,), (0,)), ((), ())), preferred_element_type=jnp.float32)

def contract_cols(left, right):
    return lax.dot_general(left, right, (((1,), (1,)), ((), ())), preferred_element_type=jnp.float32)

def layer_forward(values, gain_vec, offset):
    average = lax.optimization_barrier(jnp.mean(values, axis=-1, keepdims=True))
    centered = values - average
    inverse = lax.rsqrt(lax.optimization_barrier(jnp.mean(centered * centered, axis=-1, keepdims=True)) + EPS_NORM)
    normed = centered * inverse
    return (normed * gain_vec + offset, normed, inverse)

def layer_backward(normed, inverse, gain_vec, upstream):
    scaled = upstream * gain_vec
    mean_term = lax.optimization_barrier(jnp.mean(scaled, axis=-1, keepdims=True))
    proj_term = lax.optimization_barrier(jnp.mean(scaled * normed, axis=-1, keepdims=True))
    return inverse * (scaled - mean_term - normed * proj_term)

def partition(grid, window):
    rows_n, cols_n, depth = grid.shape
    split = grid.reshape(rows_n // window, window, cols_n // window, window, depth)
    return split.transpose(0, 2, 1, 3, 4).reshape(-1, window * window, depth)

def unpartition(windows, rows_n, cols_n, window):
    depth = windows.shape[-1]
    split = windows.reshape(rows_n // window, cols_n // window, window, window, depth)
    return split.transpose(0, 2, 1, 3, 4).reshape(rows_n, cols_n, depth)

def region_of(coords, total, window):
    return (coords >= total - window).astype(jnp.int32) + (coords >= total - window // 2).astype(jnp.int32)

def bias_from_table(table, window):
    position = jnp.arange(window * window, dtype=jnp.int32)
    row_of = position // window
    col_of = position % window
    span_len = 2 * window - 1
    lookup = (row_of[:, None] - row_of[None, :] + window - 1) * span_len + (col_of[:, None] - col_of[None, :] + window - 1)
    return 16.0 * jax.nn.sigmoid(jnp.take(table, lookup, axis=1))

def make_allowed(region_windows):
    return (region_windows[:, :, None] == region_windows[:, None, :]).astype(jnp.float32)

def attend(windows, allowed, w_qkv, b_qkv, logit_scale, head_bias, w_proj, b_proj, gain_attn, shift_attn):
    win_count, pixels, channels = windows.shape
    head_count = logit_scale.shape[0]
    head_dim = channels // head_count
    flat_rows = windows.reshape(win_count * pixels, channels)
    mixed = jnp.dot(flat_rows, w_qkv, preferred_element_type=jnp.float32) + b_qkv
    mixed = mixed.reshape(win_count, pixels, 3, head_count, head_dim)
    queries = mixed[:, :, 0]
    key_vecs = mixed[:, :, 1]
    value_low = mixed[:, :, 2].astype(jnp.bfloat16)
    query_inv = lax.rsqrt(lax.optimization_barrier(jnp.sum(queries * queries, axis=-1, keepdims=True)) + EPS_COS)
    key_inv = lax.rsqrt(lax.optimization_barrier(jnp.sum(key_vecs * key_vecs, axis=-1, keepdims=True)) + EPS_COS)
    query_unit = queries * query_inv
    key_unit = key_vecs * key_inv
    scale_vec = jnp.exp(logit_scale)[None, :, None, None]
    scores = jnp.einsum('wphd,wqhd->whpq', query_unit, key_unit, precision=HIGH) * scale_vec + head_bias[None]
    raised = jnp.exp(scores) * allowed[:, None]
    soft = raised / lax.optimization_barrier(jnp.sum(raised, axis=-1, keepdims=True))
    soft_low = soft.astype(jnp.bfloat16)
    attended = low_einsum('whpq,wqhd->wphd', soft_low, value_low)
    attended_low = attended.astype(jnp.bfloat16).reshape(win_count * pixels, channels)
    projected = jnp.dot(attended_low, w_proj, preferred_element_type=jnp.float32) + b_proj
    branch, normed, inverse = layer_forward(projected, gain_attn, shift_attn)
    output = (flat_rows.astype(jnp.float32) + branch).astype(jnp.bfloat16)
    saved = (flat_rows, query_unit, key_unit, query_inv, key_inv, value_low, soft, soft_low, attended_low, normed, inverse)
    return (output.reshape(win_count, pixels, channels), saved)

def attend_back(saved, upstream_low, w_qkv, logit_scale, w_proj, gain_attn):
    flat_rows, query_unit, key_unit, query_inv, key_inv, value_low, soft, soft_low, attended_low, normed, inverse = saved
    win_count, pixels, head_count, head_dim = query_unit.shape
    channels = head_count * head_dim
    upstream = upstream_low.astype(jnp.float32).reshape(win_count * pixels, channels)
    d_projected = layer_backward(normed, inverse, gain_attn, upstream).astype(jnp.bfloat16)
    grad_proj = contract_rows(attended_low, d_projected)
    d_attended = contract_cols(d_projected, w_proj).astype(jnp.bfloat16).reshape(win_count, pixels, head_count, head_dim)
    d_soft = low_einsum('wphd,wqhd->whpq', d_attended, value_low)
    d_value = low_einsum('whpq,wphd->wqhd', soft_low, d_attended)
    d_scores = soft * (d_soft - lax.optimization_barrier(jnp.sum(soft * d_soft, axis=-1, keepdims=True)))
    d_scaled = d_scores * jnp.exp(logit_scale)[None, :, None, None]
    d_qunit = jnp.einsum('whpq,wqhd->wphd', d_scaled, key_unit, precision=HIGH)
    d_kunit = jnp.einsum('whpq,wphd->wqhd', d_scaled, query_unit, precision=HIGH)
    d_query = query_inv * (d_qunit - query_unit * lax.optimization_barrier(jnp.sum(query_unit * d_qunit, axis=-1, keepdims=True)))
    d_key = key_inv * (d_kunit - key_unit * lax.optimization_barrier(jnp.sum(key_unit * d_kunit, axis=-1, keepdims=True)))
    d_mixed = jnp.stack([d_query, d_key, d_value], axis=2).reshape(win_count * pixels, 3 * channels).astype(jnp.bfloat16)
    grad_qkv = contract_rows(flat_rows, d_mixed)
    d_rows = contract_cols(d_mixed, w_qkv)
    d_windows = (upstream + d_rows).astype(jnp.bfloat16)
    return (d_windows.reshape(win_count, pixels, channels), grad_qkv, grad_proj)

def merge_tokens(grid):
    rows_n, cols_n, channels = grid.shape
    parts = grid.reshape(rows_n // 2, 2, cols_n // 2, 2, channels)
    return jnp.concatenate([parts[:, 0, :, 0], parts[:, 1, :, 0], parts[:, 0, :, 1], parts[:, 1, :, 1]], axis=-1)

def split_tokens(merged_grad):
    half_rows, half_cols, wide = merged_grad.shape
    channels = wide // 4
    quarter = merged_grad.reshape(half_rows, half_cols, 4, channels)
    upper = jnp.stack([quarter[:, :, 0], quarter[:, :, 2]], axis=2)
    lower = jnp.stack([quarter[:, :, 1], quarter[:, :, 3]], axis=2)
    return jnp.stack([upper, lower], axis=1).reshape(half_rows * 2, half_cols * 2, channels)

def merge_forward(grid, w_merge, gain_merge, shift_merge):
    gathered = merge_tokens(grid)
    half_rows, half_cols, wide = gathered.shape
    flat_in = gathered.reshape(half_rows * half_cols, wide)
    reduced = jnp.dot(flat_in, w_merge, preferred_element_type=jnp.float32)
    output, normed, inverse = layer_forward(reduced, gain_merge, shift_merge)
    return (output.astype(jnp.bfloat16).reshape(half_rows, half_cols, -1), (flat_in, normed, inverse))

def merge_backward(saved, upstream_low, w_merge, gain_merge):
    flat_in, normed, inverse = saved
    half_rows, half_cols, out_width = upstream_low.shape
    upstream = upstream_low.astype(jnp.float32).reshape(half_rows * half_cols, out_width)
    d_reduced = layer_backward(normed, inverse, gain_merge, upstream).astype(jnp.bfloat16)
    grad_merge = contract_rows(flat_in, d_reduced)
    d_in = contract_cols(d_reduced, w_merge).astype(jnp.bfloat16)
    return (split_tokens(d_in.reshape(half_rows, half_cols, -1)), grad_merge)

def reference(image, w_qkv, b_qkv, logit_scale, bias_table, w_proj, b_proj, gain_attn, shift_attn, w_merge, gain_merge, shift_merge, grad_out):
    rows_n, cols_n, channels = image.shape
    half = WIN // 2
    shifted = jnp.roll(image, (-half, -half), axis=(0, 1))
    win_all = partition(shifted, WIN)
    row_reg = region_of(jnp.arange(rows_n, dtype=jnp.int32), rows_n, WIN)
    col_reg = region_of(jnp.arange(cols_n, dtype=jnp.int32), cols_n, WIN)
    region = (row_reg[:, None] * 3 + col_reg[None, :])[:, :, None]
    reg_all = partition(region, WIN)[:, :, 0]
    head_bias = bias_from_table(bias_table, WIN)
    total_windows = win_all.shape[0]
    group = math.gcd(total_windows, 8)
    win_blocks = win_all.reshape(total_windows // group, group, WIN * WIN, channels)
    reg_blocks = reg_all.reshape(total_windows // group, group, WIN * WIN)

    def forward_block(pieces):
        output, saved = attend(pieces[0], make_allowed(pieces[1]), w_qkv, b_qkv, logit_scale, head_bias, w_proj, b_proj, gain_attn, shift_attn)
        return output
    out_blocks = lax.map(forward_block, (win_blocks, reg_blocks))
    shifted_out = unpartition(out_blocks.reshape(total_windows, WIN * WIN, channels), rows_n, cols_n, WIN)
    result = jnp.roll(shifted_out, (half, half), axis=(0, 1))
    merged, merge_saved = merge_forward(result, w_merge, gain_merge, shift_merge)
    d_result, grad_merge = merge_backward(merge_saved, grad_out, w_merge, gain_merge)
    d_shifted = jnp.roll(d_result, (-half, -half), axis=(0, 1))
    d_blocks = partition(d_shifted, WIN).reshape(total_windows // group, group, WIN * WIN, channels)

    def backward_block(carry, pieces):
        output, saved = attend(pieces[0], make_allowed(pieces[1]), w_qkv, b_qkv, logit_scale, head_bias, w_proj, b_proj, gain_attn, shift_attn)
        d_windows, grad_qkv, grad_proj = attend_back(saved, pieces[2], w_qkv, logit_scale, w_proj, gain_attn)
        return ((carry[0] + grad_qkv, carry[1] + grad_proj), d_windows)
    start = (jnp.zeros((channels, 3 * channels), jnp.float32), jnp.zeros((channels, channels), jnp.float32))
    grads, d_win_blocks = lax.scan(backward_block, start, (win_blocks, reg_blocks, d_blocks))
    d_image_shifted = unpartition(d_win_blocks.reshape(total_windows, WIN * WIN, channels), rows_n, cols_n, WIN)
    grad_image = jnp.roll(d_image_shifted, (half, half), axis=(0, 1))
    factor = 1.0 / math.sqrt(MERGED)
    return (merged, grad_image, (grads[0] * factor).reshape(-1), (grads[1] * factor).reshape(-1), (grad_merge * factor).reshape(-1))
```

```python
import functools
import math

import jax
import jax.numpy as jnp
from jax import lax
from jax.experimental import pallas as pl
from jax.experimental.pallas import tpu as pltpu
from jax.sharding import PartitionSpec as P

MESH = pl.DeviceIdType.MESH
F32 = jnp.float32
BF16 = jnp.bfloat16

CH = 512
HEADS = 16
HEAD = 32
TOK = 256
MTOK = 64
WIDE = 1024
EPS_NORM = 1e-05
EPS_COS = 1e-06
LOG2E = math.log2(math.e)
LN2 = math.log(2.0)

NN = (((1,), (0,)), ((), ()))
NT = (((1,), (1,)), ((), ()))
TN = (((0,), (0,)), ((), ()))


def mm(left, right, dims=NN):
    return lax.dot_general(left, right, dims, preferred_element_type=F32)


def iotas(shape):
    return (
        lax.broadcasted_iota(jnp.int32, shape, 0),
        lax.broadcasted_iota(jnp.int32, shape, 1),
    )


def onehot(cond):
    return jnp.where(cond, 1.0, 0.0).astype(BF16)


def quad_source(t):
    quad, a, b = t >> 6, (t >> 3) & 7, t & 7
    return ((quad >> 1) * 8 + a) * 16 + (quad & 1) * 8 + b


def group_source(t):
    member, quad, i, j = t >> 6, (t >> 4) & 3, (t >> 2) & 3, t & 3
    row = (quad >> 1) * 8 + 2 * i + (member & 1)
    col = (quad & 1) * 8 + 2 * j + (member >> 1)
    return row * 16 + col


def merged_source(u):
    quad, i, j = u >> 4, (u >> 2) & 3, u & 3
    return ((quad >> 1) * 4 + i) * 8 + (quad & 1) * 4 + j


def channel_source(t):
    core, parity = t >> 8, (t >> 7) & 1
    x, y, z = (t >> 5) & 3, (t >> 3) & 3, t & 7
    owner = (x >> 1) * 128 + z * 16 + y * 4 + (x & 1) * 2 + core
    return 2 * owner + parity


class Place:
    def __init__(self):
        self.c = lax.axis_index("cols")
        self.r = lax.axis_index("rows")
        self.x = (self.c // 32) * 2 + self.r // 2
        self.z = (self.c // 4) % 8
        self.y = self.c % 4
        self.k = self.r % 2
        self.coord = {"x": self.x, "y": self.y, "z": self.z}

    def beside(self, dc, dr):
        return ((self.c + dc + 64) % 64, (self.r + dr + 4) % 4)

    def sibling(self):
        return (self.c, self.r + 1 - 2 * self.k)

    def along(self, axis, step, core=None):
        core = self.k if core is None else core
        at = dict(self.coord)
        size = AXES[axis]
        at[axis] = (at[axis] + step + size) % size
        return ((at["x"] // 2) * 32 + at["z"] * 4 + at["y"], (at["x"] % 2) * 2 + core)


OPERANDS = (
    "image", "gout", "wq_in", "wp_in", "wm_in", "bq", "ls", "tab", "bp", "ga", "sa", "gm", "sm"
)
LOADS = (("image", "tile"), ("gout", "gtile"), ("wq_in", "wq"), ("wp_in", "wp"), ("wm_in", "wm"))
RESULTS = ("merged", "gimage", "gqkv", "gproj", "gmerge")
AXES = {"x": 4, "y": 4, "z": 8}
ORDERS = (("x", "y"), ("y", "x"))

SCRATCH = {
    "wq": ((CH, 3 * CH), BF16),
    "wp": ((CH, CH), BF16),
    "wm": ((4 * CH, WIDE), BF16),
    "wqT": ((3 * CH, CH), BF16),
    "wpT": ((CH, CH), BF16),
    "sentX": ((4, 64, CH), BF16),
    "gotX": ((4, 64, CH), BF16),
    "sentG": ((4, 16, WIDE), BF16),
    "gotG": ((4, 16, WIDE), BF16),
    "sentO": ((4, 16, WIDE), BF16),
    "gotO": ((4, 16, WIDE), BF16),
    "sentI": ((4, 64, CH), BF16),
    "gotI": ((4, 64, CH), BF16),
    "table": ((HEADS, 1024), F32),
    "bias": ((HEADS, TOK, TOK), F32),
    "colq": ((3 * CH, 128), F32),
    "colp": ((CH, 128), F32),
    "colg": ((CH, 128), F32),
    "cols": ((CH, 128), F32),
    "xT": ((CH, TOK), BF16),
    "qs": ((CH, TOK), BF16),
    "qu": ((CH, TOK), F32),
    "ku": ((CH, TOK), F32),
    "kb": ((CH, TOK), BF16),
    "vb": ((CH, TOK), BF16),
    "qinv": ((HEADS, TOK), F32),
    "kinv": ((HEADS, TOK), F32),
    "linv": ((HEADS, TOK), F32),
    "soft": ((HEADS, TOK, TOK), BF16),
    "att": ((CH, TOK), BF16),
    "normed": ((CH, TOK), F32),
    "dA": ((CH, TOK), BF16),
    "upT": ((CH, TOK), F32),
    "rows": ((2, TOK, TOK), BF16),
    "rowsGot": ((TOK, TOK), BF16),
    "attP": ((2, TOK, TOK), BF16),
    "attGot": ((TOK, TOK), BF16),
    "dproj": ((CH, TOK), BF16),
    "dprojGot": ((CH, TOK), BF16),
    "dmix": ((2, 3 * TOK, TOK), BF16),
    "dmixGot": ((2, 3 * TOK, TOK), BF16),
    "tile": ((TOK, CH), BF16),
    "gtile": ((MTOK, WIDE), BF16),
    "gath": ((4, 2, MTOK, 256), BF16),
    "gathAll": ((8, MTOK, 256), BF16),
    "dredAll": ((8, MTOK, WIDE), BF16),
    "ms1": ((4, 8, 16, 512), BF16),
    "mr1": ((3, 8, 16, 512), BF16),
    "ms2": ((8, 16, 512), BF16),
    "mr2": ((7, 16, 512), BF16),
    "qs1": ((2, 2, 4, 4, 4, 16, 128), BF16),
    "qr1": ((2, 2, 3, 4, 4, 16, 128), BF16),
    "qs2": ((2, 2, 4, 4, 16, 128), BF16),
    "qr2": ((2, 2, 3, 4, 16, 128), BF16),
    "qs3": ((2, 8, 16, 128), BF16),
    "qr3": ((2, 7, 16, 128), BF16),
    "fold0": ((128 * 16, 128), F32),
    "fold1": ((128 * 16, 128), F32),
}
COPIES = 96


def kernel(factor, *refs):
    names = OPERANDS + RESULTS + tuple(SCRATCH) + ("ssem", "rsem", "lsem")
    ref = dict(zip(names, refs, strict=True))
    place = Place()
    used = [0]
    pending = []

    def send(src, dst, device):
        index = used[0]
        used[0] += 1
        copy = pltpu.make_async_remote_copy(
            src_ref=src,
            dst_ref=dst,
            send_sem=ref["ssem"].at[index],
            recv_sem=ref["rsem"].at[index],
            device_id=device,
            device_id_type=MESH,
        )
        copy.start()
        pending.append(copy)
        return copy

    partners = [(dc, dr) for dc in (-1, 0, 1) for dr in (-1, 0, 1) if dc * dr >= 0 and (dc, dr) != (0, 0)]
    greeted = [place.beside(dc, dr) for dc, dr in partners] + [place.sibling()]
    for axis, size in AXES.items():
        greeted += [place.along(axis, step) for step in range(1, size)]
    greeted += [place.along("x", step, 1 - place.k) for step in range(1, 4)]
    barrier = pltpu.get_barrier_semaphore()
    for device in greeted:
        pl.semaphore_signal(barrier, inc=1, device_id=device, device_id_type=MESH)

    loads = {}
    for index, (src, dst) in enumerate(LOADS):
        loads[dst] = pltpu.make_async_copy(ref[src], ref[dst], ref["lsem"].at[index])
        loads[dst].start()

    t, n = iotas((TOK, TOK))
    to_quads = onehot(n == quad_source(t))
    from_quads = onehot(t == quad_source(n))
    groups = onehot(n == group_source(t))
    u, v = iotas((MTOK, MTOK))
    merged_quads = onehot(v == merged_source(u))
    merged_back = onehot(u == merged_source(v))
    loads["tile"].wait()
    ref["sentX"][...] = mm(to_quads, ref["tile"][...]).astype(BF16).reshape(4, 64, CH)
    loads["gtile"].wait()
    ref["sentG"][...] = mm(merged_quads, ref["gtile"][...]).astype(BF16).reshape(4, 16, WIDE)
    pl.semaphore_wait(barrier, len(greeted))

    def to_window(sent, got):
        copies = []
        for quad in (2, 1, 0):
            rh, ch = quad >> 1, quad & 1
            copies.append(
                send(ref[sent].at[quad], ref[got].at[3 - quad], place.beside(ch - 1, rh - 1))
            )
        ref[got][0] = ref[sent][3]
        return copies

    def to_image(sent, got):
        copies = []
        for quad in (3, 2, 1):
            qr, qc = quad >> 1, quad & 1
            copies.append(send(ref[sent].at[quad], ref[got].at[3 - quad], place.beside(qc, qr)))
        ref[got][3] = ref[sent][0]
        return copies

    came_x = to_window("sentX", "gotX")
    came_g = to_window("sentG", "gotG")

    def column(src, dst, size):
        ref[dst][...] = jnp.broadcast_to(ref[src][...].reshape(1, size), (128, size)).T

    column("bq", "colq", 3 * CH)
    column("bp", "colp", CH)
    column("ga", "colg", CH)
    column("sa", "cols", CH)

    def wide(name, rows=slice(None)):
        col = ref[name][rows, :]
        return jnp.concatenate([col, col], axis=1)

    build_bias(ref, place)
    loads["wq"].wait()
    loads["wp"].wait()
    for part in range(3):
        ref["wqT"][part * CH : (part + 1) * CH, :] = ref["wq"][:, part * CH : (part + 1) * CH].T
    ref["wpT"][...] = ref["wp"][...].T

    for copy in came_x:
        copy.wait_recv()
    x = mm(from_quads, ref["gotX"][...].reshape(TOK, CH)).astype(BF16)
    q = mm(ref["wqT"][:CH, :], x, NT) + wide("colq", slice(0, CH))
    k = mm(ref["wqT"][CH : 2 * CH, :], x, NT) + wide("colq", slice(CH, 2 * CH))
    val = mm(ref["wqT"][2 * CH :, :], x, NT) + wide("colq", slice(2 * CH, 3 * CH))
    ref["vb"][...] = val.astype(BF16)
    q = q.reshape(HEADS, HEAD, TOK)
    k = k.reshape(HEADS, HEAD, TOK)
    qinv = lax.rsqrt(jnp.sum(q * q, axis=1, keepdims=True) + EPS_COS)
    kinv = lax.rsqrt(jnp.sum(k * k, axis=1, keepdims=True) + EPS_COS)
    qu = (q * qinv).reshape(CH, TOK)
    ku = (k * kinv).reshape(CH, TOK)
    ref["qinv"][...] = qinv.reshape(HEADS, TOK)
    ref["kinv"][...] = kinv.reshape(HEADS, TOK)
    ref["qu"][...] = qu
    ref["ku"][...] = ku
    ref["kb"][...] = ku.astype(BF16)

    def scale_of(h):
        return jnp.exp(jnp.full((1, TOK), ref["ls"][h], F32))

    for h in range(HEADS):
        at = slice(h * HEAD, (h + 1) * HEAD)
        ref["qs"][at, :] = (qu[at, :] * (scale_of(h) * LOG2E)).astype(BF16)
    ref["xT"][...] = x.astype(F32).T.astype(BF16)

    a, b = iotas((CH, CH))
    owners = onehot(b == channel_source(a))
    ref["rows"][...] = mm(owners, x, NT).astype(BF16).reshape(2, TOK, TOK)
    came_rows = send(ref["rows"].at[1 - place.k], ref["rowsGot"], place.sibling())

    def attend(h):
        at = pl.ds(pl.multiple_of(h * HEAD, HEAD), HEAD)
        raised = jnp.exp2(mm(ref["kb"][at, :], ref["qs"][at, :], TN)) * ref["bias"][h]
        total = jnp.sum(raised, axis=0, keepdims=True)
        low = raised.astype(BF16)
        ref["soft"][h] = low
        inverse = 1.0 / total
        ref["linv"][pl.ds(h, 1), :] = inverse
        ref["att"][at, :] = (mm(ref["vb"][at, :], low) * inverse).astype(BF16)

    @pl.loop(0, HEADS // 4)
    def _(group):
        for inner in range(4):
            attend(group * 4 + inner)

    att = ref["att"][...]
    projected = mm(ref["wpT"][...], att) + wide("colp")
    average = jnp.mean(projected, axis=0, keepdims=True)
    centered = projected - average
    inverse = lax.rsqrt(jnp.mean(centered * centered, axis=0, keepdims=True) + EPS_NORM)
    normed = centered * inverse
    ref["normed"][...] = normed
    gain = wide("colg")
    branch = ref["xT"][...].astype(F32) + normed * gain + wide("cols")
    result = branch.astype(BF16)

    blocks = branch.reshape(16, 4, 8, TOK)
    ordered = jnp.concatenate([blocks[:, owner].reshape(128, TOK) for owner in range(4)], axis=0)
    ordered = ordered.astype(BF16)
    for member in range(4):
        pick = groups[member * 64 : (member + 1) * 64, :]
        part = mm(pick, ordered, NT).astype(BF16)
        lanes = slice((member & 1) * 128, (member & 1) * 128 + 128)
        for owner in range(4):
            x, core = (member >> 1) * 2 + (owner >> 1), owner & 1
            ref["gath"][x, core, :, lanes] = part[:, owner * 128 : (owner + 1) * 128]
    came_tokens = []
    ref["gathAll"][place.k] = ref["gath"][place.x, place.k]
    for step in (2, 1, 3, 0):
        for other in range(2):
            if step or other:
                core = place.k + other - 2 * other * place.k
                x = (place.x + step) % 4
                device = place.along("x", step, core)
                slot = 2 * step + place.k
                came_tokens.append(send(ref["gath"].at[x, core], ref["gathAll"].at[slot], device))
    loads["wm"].wait()
    reduced = None
    for member in range(4):
        pick = groups[member * 64 : (member + 1) * 64, :]
        gathered = mm(pick, result, NT).astype(BF16)
        term = mm(gathered, ref["wm"][member * CH : (member + 1) * CH, :])
        reduced = term if reduced is None else reduced + term
    m_average = jnp.mean(reduced, axis=-1, keepdims=True)
    m_centered = reduced - m_average
    m_inverse = lax.rsqrt(jnp.mean(m_centered * m_centered, axis=-1, keepdims=True) + EPS_NORM)
    m_normed = m_centered * m_inverse
    merged = m_normed * ref["gm"][...] + ref["sm"][...]
    ref["sentO"][...] = merged.astype(BF16).reshape(4, 16, WIDE)
    for copy in came_g:
        copy.wait_recv()
    came_o = to_image("sentO", "gotO")
    scaled = ref["gotG"][...].reshape(MTOK, WIDE).astype(F32) * ref["gm"][...]
    m_mean = jnp.mean(scaled, axis=-1, keepdims=True)
    m_proj = jnp.mean(scaled * m_normed, axis=-1, keepdims=True)
    d_reduced = (m_inverse * (scaled - m_mean - m_normed * m_proj)).astype(BF16)
    ref["dredAll"][place.k] = d_reduced
    own = ref["dredAll"].at[place.k]
    came_dred = {}
    for step in (2, 1, 3):
        slot = 2 * step + place.k
        came_dred[step] = send(own, ref["dredAll"].at[slot], place.along("x", step))
    came_tokens.append(send(own, own, place.sibling()))

    def pass_on(step):
        came_dred[step].wait_recv()
        slot = ref["dredAll"].at[2 * step + place.k]
        came_tokens.append(send(slot, slot, place.sibling()))

    upstream = None
    for member in range(4):
        d_in = mm(ref["wm"][member * CH : (member + 1) * CH, :], d_reduced, NT).astype(BF16)
        term = mm(d_in, groups[member * 64 : (member + 1) * 64, :])
        upstream = term if upstream is None else upstream + term
    ref["upT"][...] = upstream
    a_scaled = upstream * gain
    a_mean = jnp.mean(a_scaled, axis=0, keepdims=True)
    a_proj = jnp.mean(a_scaled * normed, axis=0, keepdims=True)
    ref["dproj"][...] = (inverse * (a_scaled - a_mean - normed * a_proj)).astype(BF16)
    came_dproj = send(ref["dproj"], ref["dprojGot"], place.sibling())
    ref["attP"][...] = mm(owners, att).astype(BF16).reshape(2, TOK, TOK)
    came_att = send(ref["attP"].at[1 - place.k], ref["attGot"], place.sibling())

    def start_stage(src, dst, axis):
        mine, size = place.coord[axis], AXES[axis]
        copies = []
        for step in range(1, size):
            slot = dst.at[step - 1]
            copies.append(send(src.at[(mine + step) % size], slot, place.along(axis, step)))
        return copies

    def end_stage(src, dst, axis, copies):
        total = src[place.coord[axis]].astype(F32)
        for step, copy in enumerate(copies):
            copy.wait_recv()
            total = total + dst[step].astype(F32)
        return total

    def q_refs(half, zh, stage):
        if stage == 2:
            return ref["qs3"].at[half], ref["qr3"].at[half]
        number = str(stage + 1)
        return ref["qs" + number].at[half, zh], ref["qr" + number].at[half, zh]

    def start_q(half, stage):
        if stage == 2:
            return [start_stage(*q_refs(half, 0, 2), "z")]
        return [start_stage(*q_refs(half, zh, stage), ORDERS[zh][stage]) for zh in range(2)]

    def end_q(half, stage):
        for zh in range(2):
            total = end_stage(*q_refs(half, zh, stage), ORDERS[zh][stage], q_stage[half][zh])
            if stage == 0:
                ref["qs2"][half, zh] = total.astype(BF16)
            else:
                ref["qs3"][half, 4 * zh : 4 * zh + 4] = total.astype(BF16)

    q_stage = []

    d_attended = mm(ref["wp"][...], ref["dproj"][...]).astype(BF16)
    ref["dA"][...] = d_attended

    def attend_back(h):
        at = pl.ds(pl.multiple_of(h * HEAD, HEAD), HEAD)
        linv = ref["linv"][pl.ds(h, 1), :]
        d_att = ref["dA"][at, :].astype(F32) * linv
        delta = jnp.sum(d_att * ref["att"][at, :].astype(F32), axis=0, keepdims=True)
        d_low = d_att.astype(BF16)
        soft = ref["soft"][h]
        d_soft = mm(ref["vb"][at, :], d_low, TN)
        d_scores = (soft.astype(F32) * (d_soft - delta)).astype(BF16)
        scale = scale_of(h)
        d_value = mm(d_low, soft, NT)
        d_qu = mm(ref["kb"][at, :], d_scores) * scale
        d_ku = mm(ref["qs"][at, :], d_scores, NT) * LN2
        q_unit, k_unit = ref["qu"][at, :], ref["ku"][at, :]
        d_q = ref["qinv"][pl.ds(h, 1), :] * (
            d_qu - q_unit * jnp.sum(q_unit * d_qu, axis=0, keepdims=True)
        )
        d_k = ref["kinv"][pl.ds(h, 1), :] * (
            d_ku - k_unit * jnp.sum(k_unit * d_ku, axis=0, keepdims=True)
        )
        for part, values in enumerate((d_q, d_k, d_value)):
            rows = pl.ds(pl.multiple_of(part * 256 + (h & 7) * HEAD, HEAD), HEAD)
            ref["dmix"][h >> 3, rows, :] = values.astype(BF16)

    folds = (ref["fold0"], ref["fold1"])

    def put(half, unit, values):
        for lane in range(2):
            part = values[:, lane * 128 : (lane + 1) * 128]
            folds[half][pl.ds(unit + lane, 128, stride=16), :] = part

    came_mix = []
    for half in range(2):

        @pl.loop(half * 2, half * 2 + 2)
        def _(group):
            for inner in range(4):
                attend_back(group * 4 + inner)

        came_mix.append(send(ref["dmix"].at[half], ref["dmixGot"].at[half], place.sibling()))
        if half == 0:
            pass_on(1)
            pass_on(3)
            came_rows.wait_recv()
            came_att.wait_recv()
            came_dproj.wait_recv()
            own_att = ref["attP"][place.k]
            for piece in range(2):
                cols = slice(piece * 256, (piece + 1) * 256)
                part = mm(own_att, ref["dproj"][cols, :], NT)
                part = part + mm(ref["attGot"][...], ref["dprojGot"][cols, :], NT)
                put(0, 12 + 2 * piece, part[:128])
                put(1, 12 + 2 * piece, part[128:])
        else:
            pass_on(2)
            d_rows = None
            for block in range(6):
                cols = slice((block % 3) * 512 + (block // 3) * 256, (block % 3) * 512 + (block // 3) * 256 + 256)
                rows = slice((block % 3) * 256, (block % 3) * 256 + 256)
                term = mm(ref["wq"][:, cols], ref["dmix"][block // 3, rows, :])
                d_rows = term if d_rows is None else d_rows + term
            d_image = (ref["upT"][...] + d_rows).astype(BF16)
            ref["sentI"][...] = mm(to_quads, d_image, NT).astype(BF16).reshape(4, 64, CH)
            came_i = to_image("sentI", "gotI")
        came_mix[half].wait_recv()
        own_rows = ref["rows"][place.k]
        for part in range(3):
            cols = slice(part * 256, (part + 1) * 256)
            values = mm(own_rows, ref["dmix"][half, cols, :], NT)
            values = values + mm(ref["rowsGot"][...], ref["dmixGot"][half, cols, :], NT)
            put(half, 2 * part, values[:128])
            put(half, 6 + 2 * part, values[128:])
        for first in range(4):
            for second in range(4):
                at = pl.ds((first * 4 + second) * 128, 128)
                share = folds[half][at, :].astype(BF16).reshape(8, 16, 128)
                ref["qs1"][half, 0, first, second] = share[:4]
                ref["qs1"][half, 1, second, first] = share[4:]
        q_stage.append(start_q(half, 0))
    for copy in came_tokens:
        copy.wait_recv()
    tokens = ref["gathAll"][...].reshape(8 * MTOK, 256)
    grads = mm(tokens, ref["dredAll"][...].reshape(8 * MTOK, WIDE), TN).reshape(8, 4, 8, WIDE)
    shares = jnp.concatenate([grads[..., :512], grads[..., 512:]], axis=2).astype(BF16)
    for y in range(4):
        ref["ms1"][y] = shares[:, y]
    m_copies = start_stage(ref["ms1"], ref["mr1"], "y")

    end_q(0, 0)
    q_stage[0] = start_q(0, 1)
    end_q(1, 0)
    q_stage[1] = start_q(1, 1)

    for copy in came_o:
        copy.wait_recv()
    ref["merged"][...] = mm(merged_back, ref["gotO"][...].reshape(MTOK, WIDE)).astype(BF16)

    end_q(0, 1)
    q_stage[0] = start_q(0, 2)
    end_q(1, 1)
    q_stage[1] = start_q(1, 2)
    ref["ms2"][...] = end_stage(ref["ms1"], ref["mr1"], "y", m_copies).astype(BF16)
    m_copies = start_stage(ref["ms2"], ref["mr2"], "z")

    for copy in came_i:
        copy.wait_recv()
    ref["gimage"][...] = mm(from_quads, ref["gotI"][...].reshape(TOK, CH)).astype(BF16)

    for half in range(2):
        total = end_stage(*q_refs(half, 0, 2), "z", q_stage[half][0]) * factor
        for parity in range(2):
            for part in range(3):
                row, unit = parity * 12 + part * 4 + half * 2, parity * 6 + part * 2
                ref["gqkv"][row : row + 2, :] = total[unit : unit + 2]
        ref["gproj"][half * 4 : half * 4 + 4, :] = total[12:]
    total = end_stage(ref["ms2"], ref["mr2"], "z", m_copies) * factor
    for fold in range(2):
        for lane in range(4):
            part = total[fold * 8 : fold * 8 + 8, lane * 128 : (lane + 1) * 128]
            ref["gmerge"][pl.ds(fold * 4 + lane, 8, stride=8), :] = part
    for copy in pending:
        copy.wait_send()
    assert used[0] <= COPIES


def build_bias(ref, place):
    ref["table"][...] = jnp.zeros((HEADS, 1024), F32)
    ref["table"][:, :961] = (16.0 * LOG2E) * jax.nn.sigmoid(ref["tab"][...])
    high = ref["table"][...].astype(BF16).astype(F32)
    low = ref["table"][...] - high
    k = lax.broadcasted_iota(jnp.int32, (HEAD, 1024), 1)
    b = lax.broadcasted_iota(jnp.int32, (HEAD, 1024), 0)
    chosen = jnp.where((k - 31 * ((k * 2115) >> 16)) == 30 - b, 1.0, 0.0)
    k, lane = iotas((1024, 512))
    spread = onehot(((k * 2115) >> 16) == (lane >> 4))
    terms = None
    for part in (high, low):
        left = (part[:, None, :] * chosen[None]).reshape(HEADS * HEAD, 1024).astype(BF16)
        term = mm(left, spread)
        terms = term if terms is None else terms + term
    lane = lax.broadcasted_iota(jnp.int32, (HEAD, 512), 1)
    shift = 15 - (lane & 15)
    q, p = iotas((TOK, TOK))
    last_row = place.r == 3
    last_col = place.c == 63
    row_cut = jnp.where((q >> 7) != (p >> 7), jnp.where(last_row, 0.0, 1.0), 1.0)
    col_cut = jnp.where(((q >> 3) & 1) != ((p >> 3) & 1), jnp.where(last_col, 0.0, 1.0), 1.0)
    allowed = row_cut * col_cut
    for h in range(HEADS):
        rows = terms[h * HEAD : (h + 1) * HEAD, :]
        for bit in range(4):
            moved = pltpu.roll(rows, HEAD - (1 << bit), 0)
            rows = jnp.where(((shift >> bit) & 1) == 1, moved, rows)
        rows = jnp.exp2(rows[:16])
        for turn in range(8):
            turned = rows if turn == 0 else pltpu.roll(rows, 512 - 16 * turn, 1)
            for whole in range(2):
                row = 15 - (whole * 8 + turn)
                at = slice(row * 16, (row + 1) * 16)
                ref["bias"][h, at, :] = turned[:, whole * 128 : whole * 128 + 256] * allowed[at, :]


def copy_out(*refs):
    count = len(refs) // 2
    for index in range(count):
        refs[count + index][...] = refs[index][...]


def hand_over(arrays):
    vmem = pl.BlockSpec(memory_space=pltpu.VMEM)
    return pl.pallas_call(
        copy_out,
        name="results",
        out_shape=tuple(jax.ShapeDtypeStruct(a.shape, a.dtype) for a in arrays),
        in_specs=[vmem] * len(arrays),
        out_specs=(vmem,) * len(arrays),
    )(*arrays)


def per_device(
    image,
    w_qkv,
    b_qkv,
    logit_scale,
    bias_table,
    w_proj,
    b_proj,
    gain_attn,
    shift_attn,
    w_merge,
    gain_merge,
    shift_merge,
    grad_out,
):
    vmem = pl.BlockSpec(memory_space=pltpu.VMEM)
    smem = pl.BlockSpec(memory_space=pltpu.SMEM)
    anywhere = pl.BlockSpec(memory_space=pl.ANY)
    factor = 1.0 / math.sqrt(16384)
    outs = pl.pallas_call(
        functools.partial(kernel, factor),
        name="block",
        out_shape=(
            jax.ShapeDtypeStruct((MTOK, WIDE), BF16),
            jax.ShapeDtypeStruct((TOK, CH), BF16),
            jax.ShapeDtypeStruct((24, 128), F32),
            jax.ShapeDtypeStruct((8, 128), F32),
            jax.ShapeDtypeStruct((64, 128), F32),
        ),
        in_specs=[anywhere] * 5 + [vmem, smem] + [vmem] * 6,
        out_specs=(vmem,) * 5,
        scratch_shapes=[pltpu.VMEM(shape, dtype) for shape, dtype in SCRATCH.values()]
        + [
            pltpu.SemaphoreType.DMA((COPIES,)),
            pltpu.SemaphoreType.DMA((COPIES,)),
            pltpu.SemaphoreType.DMA((len(LOADS),)),
        ],
        compiler_params=pltpu.CompilerParams(
            collective_id=0, has_side_effects=True, vmem_limit_bytes=60 * 2**20
        ),
    )(
        image.reshape(TOK, CH),
        grad_out.reshape(MTOK, WIDE),
        w_qkv,
        w_proj,
        w_merge,
        b_qkv,
        logit_scale,
        bias_table,
        b_proj.reshape(1, -1),
        gain_attn.reshape(1, -1),
        shift_attn.reshape(1, -1),
        gain_merge.reshape(1, -1),
        shift_merge.reshape(1, -1),
    )
    merged, gimage, gqkv, gproj, gmerge = hand_over(outs)
    return (
        merged.reshape(8, 8, WIDE),
        gimage.reshape(16, 16, CH),
        gqkv.reshape(-1),
        gproj.reshape(-1),
        gmerge.reshape(-1),
    )


def solution(mesh):
    whole = P()
    tiles = P("rows", "cols", None)
    flat = P(("cols", "rows"))
    return jax.shard_map(
        per_device,
        mesh=mesh,
        in_specs=(tiles,) + (whole,) * 11 + (tiles,),
        out_specs=(tiles, tiles, flat, flat, flat),
        check_vma=False,
    )
```

```python
import functools
import math

import jax
import jax.numpy as jnp
from jax import lax
from jax.experimental import pallas as pl
from jax.experimental.pallas import tpu as pltpu
from jax.sharding import PartitionSpec as P

MESH = pl.DeviceIdType.MESH
F32 = jnp.float32
BF16 = jnp.bfloat16

CH = 512
HEADS = 16
HEAD = 32
TOK = 256
MTOK = 64
WIDE = 1024
EPS_NORM = 1e-05
EPS_COS = 1e-06
LOG2E = math.log2(math.e)
LN2 = math.log(2.0)

NN = (((1,), (0,)), ((), ()))
NT = (((1,), (1,)), ((), ()))
TN = (((0,), (0,)), ((), ()))


def mm(left, right, dims=NN):
    return lax.dot_general(left, right, dims, preferred_element_type=F32)


def iotas(shape):
    return (
        lax.broadcasted_iota(jnp.int32, shape, 0),
        lax.broadcasted_iota(jnp.int32, shape, 1),
    )


def onehot(cond):
    return jnp.where(cond, 1.0, 0.0).astype(BF16)


def quad_source(t):
    quad, a, b = t >> 6, (t >> 3) & 7, t & 7
    return ((quad >> 1) * 8 + a) * 16 + (quad & 1) * 8 + b


def group_source(t):
    member, quad, i, j = t >> 6, (t >> 4) & 3, (t >> 2) & 3, t & 3
    row = (quad >> 1) * 8 + 2 * i + (member & 1)
    col = (quad & 1) * 8 + 2 * j + (member >> 1)
    return row * 16 + col


def merged_source(u):
    quad, i, j = u >> 4, (u >> 2) & 3, u & 3
    return ((quad >> 1) * 4 + i) * 8 + (quad & 1) * 4 + j


def channel_source(t):
    core, parity = t >> 8, (t >> 7) & 1
    x, y, z = (t >> 5) & 3, (t >> 3) & 3, t & 7
    owner = (x >> 1) * 128 + z * 16 + y * 4 + (x & 1) * 2 + core
    return 2 * owner + parity


class Place:
    def __init__(self):
        self.c = lax.axis_index("cols")
        self.r = lax.axis_index("rows")
        self.x = (self.c // 32) * 2 + self.r // 2
        self.z = (self.c // 4) % 8
        self.y = self.c % 4
        self.k = self.r % 2
        self.coord = {"x": self.x, "y": self.y, "z": self.z}

    def beside(self, dc, dr):
        return ((self.c + dc + 64) % 64, (self.r + dr + 4) % 4)

    def sibling(self):
        return (self.c, self.r + 1 - 2 * self.k)

    def along(self, axis, step, core=None):
        core = self.k if core is None else core
        at = dict(self.coord)
        size = AXES[axis]
        at[axis] = (at[axis] + step + size) % size
        return ((at["x"] // 2) * 32 + at["z"] * 4 + at["y"], (at["x"] % 2) * 2 + core)


OPERANDS = (
    "image", "gout", "wq_in", "wp_in", "wm_in", "bq", "ls", "tab", "bp", "ga", "sa", "gm", "sm"
)
LOADS = (("image", "tile"), ("gout", "gtile"), ("wq_in", "wq"), ("wp_in", "wp"), ("wm_in", "wm"))
RESULTS = ("merged", "gimage", "gqkv", "gproj", "gmerge")
AXES = {"x": 4, "y": 4, "z": 8}
ORDERS = (("x", "y"), ("y", "x"))

SCRATCH = {
    "wq": ((CH, 3 * CH), BF16),
    "wp": ((CH, CH), BF16),
    "wm": ((4 * CH, WIDE), BF16),
    "wqT": ((3 * CH, CH), BF16),
    "wpT": ((CH, CH), BF16),
    "sentX": ((4, 64, CH), BF16),
    "gotX": ((4, 64, CH), BF16),
    "sentG": ((4, 16, WIDE), BF16),
    "gotG": ((4, 16, WIDE), BF16),
    "sentO": ((4, 16, WIDE), BF16),
    "gotO": ((4, 16, WIDE), BF16),
    "sentI": ((4, 64, CH), BF16),
    "gotI": ((4, 64, CH), BF16),
    "table": ((HEADS, 1024), F32),
    "bias": ((HEADS, TOK, TOK), F32),
    "colq": ((3 * CH, 128), F32),
    "colp": ((CH, 128), F32),
    "colg": ((CH, 128), F32),
    "cols": ((CH, 128), F32),
    "xT": ((CH, TOK), BF16),
    "qs": ((CH, TOK), BF16),
    "qu": ((CH, TOK), F32),
    "ku": ((CH, TOK), F32),
    "kb": ((CH, TOK), BF16),
    "vb": ((CH, TOK), BF16),
    "qinv": ((HEADS, TOK), F32),
    "kinv": ((HEADS, TOK), F32),
    "linv": ((HEADS, TOK), F32),
    "soft": ((HEADS, TOK, TOK), BF16),
    "att": ((CH, TOK), BF16),
    "normed": ((CH, TOK), F32),
    "dA": ((CH, TOK), BF16),
    "upT": ((CH, TOK), F32),
    "rows": ((2, TOK, TOK), BF16),
    "rowsGot": ((TOK, TOK), BF16),
    "attP": ((2, TOK, TOK), BF16),
    "attGot": ((TOK, TOK), BF16),
    "dproj": ((CH, TOK), BF16),
    "dprojGot": ((CH, TOK), BF16),
    "dmix": ((2, 3 * TOK, TOK), BF16),
    "dmixGot": ((2, 3 * TOK, TOK), BF16),
    "tile": ((TOK, CH), BF16),
    "gtile": ((MTOK, WIDE), BF16),
    "gath": ((4, 2, MTOK, 256), BF16),
    "gathAll": ((8, MTOK, 256), BF16),
    "dredAll": ((2, 8, MTOK, CH), BF16),
    "ms1": ((2, 4, 8, 16, 256), BF16),
    "mr1": ((2, 3, 8, 16, 256), BF16),
    "ms2": ((2, 8, 16, 256), BF16),
    "mr2": ((2, 7, 16, 256), BF16),
    "qs1": ((2, 2, 4, 4, 4, 16, 128), BF16),
    "qr1": ((2, 2, 3, 4, 4, 16, 128), BF16),
    "qs2": ((2, 2, 4, 4, 16, 128), BF16),
    "qr2": ((2, 2, 3, 4, 16, 128), BF16),
    "qs3": ((2, 8, 16, 128), BF16),
    "qr3": ((2, 7, 16, 128), BF16),
    "fold0": ((128 * 16, 128), F32),
    "fold1": ((128 * 16, 128), F32),
}
COPIES = 96


def kernel(factor, *refs):
    names = OPERANDS + RESULTS + tuple(SCRATCH) + ("ssem", "rsem", "lsem")
    ref = dict(zip(names, refs, strict=True))
    place = Place()
    used = [0]
    pending = []

    def send(src, dst, device):
        index = used[0]
        used[0] += 1
        copy = pltpu.make_async_remote_copy(
            src_ref=src,
            dst_ref=dst,
            send_sem=ref["ssem"].at[index],
            recv_sem=ref["rsem"].at[index],
            device_id=device,
            device_id_type=MESH,
        )
        copy.start()
        pending.append(copy)
        return copy

    partners = [(dc, dr) for dc in (-1, 0, 1) for dr in (-1, 0, 1) if dc * dr >= 0 and (dc, dr) != (0, 0)]
    greeted = [place.beside(dc, dr) for dc, dr in partners] + [place.sibling()]
    for axis, size in AXES.items():
        greeted += [place.along(axis, step) for step in range(1, size)]
    greeted += [place.along("x", step, 1 - place.k) for step in range(1, 4)]
    barrier = pltpu.get_barrier_semaphore()
    for device in greeted:
        pl.semaphore_signal(barrier, inc=1, device_id=device, device_id_type=MESH)

    loads = {}
    for index, (src, dst) in enumerate(LOADS):
        loads[dst] = pltpu.make_async_copy(ref[src], ref[dst], ref["lsem"].at[index])
        loads[dst].start()

    t, n = iotas((TOK, TOK))
    to_quads = onehot(n == quad_source(t))
    from_quads = onehot(t == quad_source(n))
    groups = onehot(n == group_source(t))
    u, v = iotas((MTOK, MTOK))
    merged_quads = onehot(v == merged_source(u))
    merged_back = onehot(u == merged_source(v))
    loads["tile"].wait()
    ref["sentX"][...] = mm(to_quads, ref["tile"][...]).astype(BF16).reshape(4, 64, CH)
    loads["gtile"].wait()
    ref["sentG"][...] = mm(merged_quads, ref["gtile"][...]).astype(BF16).reshape(4, 16, WIDE)
    pl.semaphore_wait(barrier, len(greeted))

    def to_window(sent, got):
        copies = []
        for quad in (2, 1, 0):
            rh, ch = quad >> 1, quad & 1
            copies.append(
                send(ref[sent].at[quad], ref[got].at[3 - quad], place.beside(ch - 1, rh - 1))
            )
        ref[got][0] = ref[sent][3]
        return copies

    def to_image(sent, got):
        copies = []
        for quad in (3, 2, 1):
            qr, qc = quad >> 1, quad & 1
            copies.append(send(ref[sent].at[quad], ref[got].at[3 - quad], place.beside(qc, qr)))
        ref[got][3] = ref[sent][0]
        return copies

    came_x = to_window("sentX", "gotX")
    came_g = to_window("sentG", "gotG")

    def column(src, dst, size):
        ref[dst][...] = jnp.broadcast_to(ref[src][...].reshape(1, size), (128, size)).T

    column("bq", "colq", 3 * CH)
    column("bp", "colp", CH)
    column("ga", "colg", CH)
    column("sa", "cols", CH)

    def wide(name, rows=slice(None)):
        col = ref[name][rows, :]
        return jnp.concatenate([col, col], axis=1)

    build_bias(ref, place)
    loads["wq"].wait()
    loads["wp"].wait()
    for part in range(3):
        ref["wqT"][part * CH : (part + 1) * CH, :] = ref["wq"][:, part * CH : (part + 1) * CH].T
    ref["wpT"][...] = ref["wp"][...].T

    for copy in came_x:
        copy.wait_recv()
    x = mm(from_quads, ref["gotX"][...].reshape(TOK, CH)).astype(BF16)
    q = mm(ref["wqT"][:CH, :], x, NT) + wide("colq", slice(0, CH))
    k = mm(ref["wqT"][CH : 2 * CH, :], x, NT) + wide("colq", slice(CH, 2 * CH))
    val = mm(ref["wqT"][2 * CH :, :], x, NT) + wide("colq", slice(2 * CH, 3 * CH))
    ref["vb"][...] = val.astype(BF16)
    q = q.reshape(HEADS, HEAD, TOK)
    k = k.reshape(HEADS, HEAD, TOK)
    qinv = lax.rsqrt(jnp.sum(q * q, axis=1, keepdims=True) + EPS_COS)
    kinv = lax.rsqrt(jnp.sum(k * k, axis=1, keepdims=True) + EPS_COS)
    qu = (q * qinv).reshape(CH, TOK)
    ku = (k * kinv).reshape(CH, TOK)
    ref["qinv"][...] = qinv.reshape(HEADS, TOK)
    ref["kinv"][...] = kinv.reshape(HEADS, TOK)
    ref["qu"][...] = qu
    ref["ku"][...] = ku
    ref["kb"][...] = ku.astype(BF16)

    def scale_of(h):
        return jnp.exp(jnp.full((1, TOK), ref["ls"][h], F32))

    for h in range(HEADS):
        at = slice(h * HEAD, (h + 1) * HEAD)
        ref["qs"][at, :] = (qu[at, :] * (scale_of(h) * LOG2E)).astype(BF16)
    ref["xT"][...] = x.astype(F32).T.astype(BF16)

    a, b = iotas((CH, CH))
    owners = onehot(b == channel_source(a))
    ref["rows"][...] = mm(owners, x, NT).astype(BF16).reshape(2, TOK, TOK)
    came_rows = send(ref["rows"].at[1 - place.k], ref["rowsGot"], place.sibling())

    def attend(h):
        at = pl.ds(pl.multiple_of(h * HEAD, HEAD), HEAD)
        raised = jnp.exp2(mm(ref["kb"][at, :], ref["qs"][at, :], TN)) * ref["bias"][h]
        total = jnp.sum(raised, axis=0, keepdims=True)
        low = raised.astype(BF16)
        ref["soft"][h] = low
        inverse = 1.0 / total
        ref["linv"][pl.ds(h, 1), :] = inverse
        ref["att"][at, :] = (mm(ref["vb"][at, :], low) * inverse).astype(BF16)

    for h in range(HEADS):
        attend(h)

    att = ref["att"][...]
    projected = mm(ref["wpT"][...], att) + wide("colp")
    average = jnp.mean(projected, axis=0, keepdims=True)
    centered = projected - average
    inverse = lax.rsqrt(jnp.mean(centered * centered, axis=0, keepdims=True) + EPS_NORM)
    normed = centered * inverse
    ref["normed"][...] = normed
    gain = wide("colg")
    branch = ref["xT"][...].astype(F32) + normed * gain + wide("cols")
    result = branch.astype(BF16)

    blocks = branch.reshape(16, 4, 8, TOK)
    ordered = jnp.concatenate([blocks[:, owner].reshape(128, TOK) for owner in range(4)], axis=0)
    ordered = ordered.astype(BF16)
    for member in range(4):
        pick = groups[member * 64 : (member + 1) * 64, :]
        part = mm(pick, ordered, NT).astype(BF16)
        lanes = slice((member & 1) * 128, (member & 1) * 128 + 128)
        for owner in range(4):
            x, core = (member >> 1) * 2 + (owner >> 1), owner & 1
            ref["gath"][x, core, :, lanes] = part[:, owner * 128 : (owner + 1) * 128]
    came_tokens = []
    ref["gathAll"][place.k] = ref["gath"][place.x, place.k]
    for step in (2, 1, 3, 0):
        for other in range(2):
            if step or other:
                core = place.k + other - 2 * other * place.k
                x = (place.x + step) % 4
                device = place.along("x", step, core)
                slot = 2 * step + place.k
                came_tokens.append(send(ref["gath"].at[x, core], ref["gathAll"].at[slot], device))
    loads["wm"].wait()
    reduced = None
    for member in range(4):
        pick = groups[member * 64 : (member + 1) * 64, :]
        gathered = mm(pick, result, NT).astype(BF16)
        term = mm(gathered, ref["wm"][member * CH : (member + 1) * CH, :])
        reduced = term if reduced is None else reduced + term
    m_average = jnp.mean(reduced, axis=-1, keepdims=True)
    m_centered = reduced - m_average
    m_inverse = lax.rsqrt(jnp.mean(m_centered * m_centered, axis=-1, keepdims=True) + EPS_NORM)
    m_normed = m_centered * m_inverse
    merged = m_normed * ref["gm"][...] + ref["sm"][...]
    ref["sentO"][...] = merged.astype(BF16).reshape(4, 16, WIDE)
    for copy in came_g:
        copy.wait_recv()
    came_o = to_image("sentO", "gotO")
    scaled = ref["gotG"][...].reshape(MTOK, WIDE).astype(F32) * ref["gm"][...]
    m_mean = jnp.mean(scaled, axis=-1, keepdims=True)
    m_proj = jnp.mean(scaled * m_normed, axis=-1, keepdims=True)
    d_reduced = (m_inverse * (scaled - m_mean - m_normed * m_proj)).astype(BF16)
    came_dred = {}
    came_half = [[], []]
    for part in range(2):
        ref["dredAll"][part, place.k] = d_reduced[:, part * CH : (part + 1) * CH]
        own = ref["dredAll"].at[part, place.k]
        for step in (2, 1, 3):
            slot = ref["dredAll"].at[part, 2 * step + place.k]
            came_dred[part, step] = send(own, slot, place.along("x", step))
        came_half[part].append(send(own, own, place.sibling()))

    def pass_on(part):
        for step in (1, 3, 2):
            came_dred[part, step].wait_recv()
            slot = ref["dredAll"].at[part, 2 * step + place.k]
            came_half[part].append(send(slot, slot, place.sibling()))

    def merge_grads(part):
        if part == 0:
            for copy in came_tokens:
                copy.wait_recv()
        for copy in came_half[part]:
            copy.wait_recv()
        tokens = ref["gathAll"][...].reshape(8 * MTOK, 256)
        grads = mm(tokens, ref["dredAll"][part].reshape(8 * MTOK, CH), TN).reshape(8, 4, 8, CH)
        shares = jnp.concatenate([grads[..., :256], grads[..., 256:]], axis=2).astype(BF16)
        for y in range(4):
            ref["ms1"][part, y] = shares[:, y]
        return start_stage(ref["ms1"].at[part], ref["mr1"].at[part], "y")

    d_in = [
        mm(d_reduced, ref["wm"][member * CH : (member + 1) * CH, :], NT).astype(BF16)
        for member in range(4)
    ]
    upstream = mm(jnp.concatenate(d_in, axis=0), groups, TN)
    ref["upT"][...] = upstream
    a_scaled = upstream * gain
    a_mean = jnp.mean(a_scaled, axis=0, keepdims=True)
    a_proj = jnp.mean(a_scaled * normed, axis=0, keepdims=True)
    ref["dproj"][...] = (inverse * (a_scaled - a_mean - normed * a_proj)).astype(BF16)
    came_dproj = send(ref["dproj"], ref["dprojGot"], place.sibling())
    ref["attP"][...] = mm(owners, att).astype(BF16).reshape(2, TOK, TOK)
    came_att = send(ref["attP"].at[1 - place.k], ref["attGot"], place.sibling())

    def start_stage(src, dst, axis):
        mine, size = place.coord[axis], AXES[axis]
        copies = []
        for step in range(1, size):
            slot = dst.at[step - 1]
            copies.append(send(src.at[(mine + step) % size], slot, place.along(axis, step)))
        return copies

    def end_stage(src, dst, axis, copies):
        total = src[place.coord[axis]].astype(F32)
        for step, copy in enumerate(copies):
            copy.wait_recv()
            total = total + dst[step].astype(F32)
        return total

    def q_refs(half, zh, stage):
        if stage == 2:
            return ref["qs3"].at[half], ref["qr3"].at[half]
        number = str(stage + 1)
        return ref["qs" + number].at[half, zh], ref["qr" + number].at[half, zh]

    def start_q(half, stage):
        if stage == 2:
            return [start_stage(*q_refs(half, 0, 2), "z")]
        return [start_stage(*q_refs(half, zh, stage), ORDERS[zh][stage]) for zh in range(2)]

    def end_q(half, stage):
        for zh in range(2):
            total = end_stage(*q_refs(half, zh, stage), ORDERS[zh][stage], q_stage[half][zh])
            if stage == 0:
                ref["qs2"][half, zh] = total.astype(BF16)
            else:
                ref["qs3"][half, 4 * zh : 4 * zh + 4] = total.astype(BF16)

    q_stage = []
    m_copies = []

    def second_m(part):
        ref["ms2"][part] = end_stage(
            ref["ms1"].at[part], ref["mr1"].at[part], "y", m_copies[part]
        ).astype(BF16)
        m_copies[part] = start_stage(ref["ms2"].at[part], ref["mr2"].at[part], "z")

    d_attended = mm(ref["wp"][...], ref["dproj"][...]).astype(BF16)
    ref["dA"][...] = d_attended

    def attend_back(h):
        at = pl.ds(pl.multiple_of(h * HEAD, HEAD), HEAD)
        linv = ref["linv"][pl.ds(h, 1), :]
        d_att = ref["dA"][at, :].astype(F32) * linv
        delta = jnp.sum(d_att * ref["att"][at, :].astype(F32), axis=0, keepdims=True)
        d_low = d_att.astype(BF16)
        soft = ref["soft"][h]
        d_soft = mm(ref["vb"][at, :], d_low, TN)
        d_scores = (soft.astype(F32) * (d_soft - delta)).astype(BF16)
        scale = scale_of(h)
        d_value = mm(d_low, soft, NT)
        d_qu = mm(ref["kb"][at, :], d_scores) * scale
        d_ku = mm(ref["qs"][at, :], d_scores, NT) * LN2
        q_unit, k_unit = ref["qu"][at, :], ref["ku"][at, :]
        d_q = ref["qinv"][pl.ds(h, 1), :] * (
            d_qu - q_unit * jnp.sum(q_unit * d_qu, axis=0, keepdims=True)
        )
        d_k = ref["kinv"][pl.ds(h, 1), :] * (
            d_ku - k_unit * jnp.sum(k_unit * d_ku, axis=0, keepdims=True)
        )
        for part, values in enumerate((d_q, d_k, d_value)):
            rows = pl.ds(pl.multiple_of(part * 256 + (h & 7) * HEAD, HEAD), HEAD)
            ref["dmix"][h >> 3, rows, :] = values.astype(BF16)

    folds = (ref["fold0"], ref["fold1"])

    def put(half, unit, values):
        for lane in range(2):
            part = values[:, lane * 128 : (lane + 1) * 128]
            folds[half][pl.ds(unit + lane, 128, stride=16), :] = part

    came_mix = []
    for half in range(2):

        for h in range(8):
            attend_back(half * 8 + h)

        came_mix.append(send(ref["dmix"].at[half], ref["dmixGot"].at[half], place.sibling()))
        if half == 0:
            pass_on(0)
            came_rows.wait_recv()
            came_att.wait_recv()
            came_dproj.wait_recv()
            own_att = ref["attP"][place.k]
            for piece in range(2):
                cols = slice(piece * 256, (piece + 1) * 256)
                part = mm(own_att, ref["dproj"][cols, :], NT)
                part = part + mm(ref["attGot"][...], ref["dprojGot"][cols, :], NT)
                put(0, 12 + 2 * piece, part[:128])
                put(1, 12 + 2 * piece, part[128:])
        else:
            m_copies.append(merge_grads(0))
            pass_on(1)
            d_rows = None
            for block in range(6):
                cols = slice((block % 3) * 512 + (block // 3) * 256, (block % 3) * 512 + (block // 3) * 256 + 256)
                rows = slice((block % 3) * 256, (block % 3) * 256 + 256)
                term = mm(ref["wq"][:, cols], ref["dmix"][block // 3, rows, :])
                d_rows = term if d_rows is None else d_rows + term
            d_image = (ref["upT"][...] + d_rows).astype(BF16)
            ref["sentI"][...] = mm(to_quads, d_image, NT).astype(BF16).reshape(4, 64, CH)
            came_i = to_image("sentI", "gotI")
        came_mix[half].wait_recv()
        own_rows = ref["rows"][place.k]
        for part in range(3):
            cols = slice(part * 256, (part + 1) * 256)
            values = mm(own_rows, ref["dmix"][half, cols, :], NT)
            values = values + mm(ref["rowsGot"][...], ref["dmixGot"][half, cols, :], NT)
            put(half, 2 * part, values[:128])
            put(half, 6 + 2 * part, values[128:])
        for first in range(4):
            for second in range(4):
                at = pl.ds((first * 4 + second) * 128, 128)
                share = folds[half][at, :].astype(BF16).reshape(8, 16, 128)
                ref["qs1"][half, 0, first, second] = share[:4]
                ref["qs1"][half, 1, second, first] = share[4:]
        q_stage.append(start_q(half, 0))
    m_copies.append(merge_grads(1))

    end_q(0, 0)
    q_stage[0] = start_q(0, 1)
    end_q(1, 0)
    q_stage[1] = start_q(1, 1)
    second_m(0)

    for copy in came_o:
        copy.wait_recv()
    ref["merged"][...] = mm(merged_back, ref["gotO"][...].reshape(MTOK, WIDE)).astype(BF16)

    end_q(0, 1)
    q_stage[0] = start_q(0, 2)
    end_q(1, 1)
    q_stage[1] = start_q(1, 2)
    second_m(1)

    for copy in came_i:
        copy.wait_recv()
    ref["gimage"][...] = mm(from_quads, ref["gotI"][...].reshape(TOK, CH)).astype(BF16)

    for half in range(2):
        total = end_stage(*q_refs(half, 0, 2), "z", q_stage[half][0]) * factor
        for parity in range(2):
            for part in range(3):
                row, unit = parity * 12 + part * 4 + half * 2, parity * 6 + part * 2
                ref["gqkv"][row : row + 2, :] = total[unit : unit + 2]
        ref["gproj"][half * 4 : half * 4 + 4, :] = total[12:]
    for half in range(2):
        total = end_stage(ref["ms2"].at[half], ref["mr2"].at[half], "z", m_copies[half]) * factor
        for fold in range(2):
            for lane in range(2):
                part = total[fold * 8 : fold * 8 + 8, lane * 128 : (lane + 1) * 128]
                ref["gmerge"][pl.ds(half * 4 + fold * 2 + lane, 8, stride=8), :] = part
    for copy in pending:
        copy.wait_send()
    assert used[0] <= COPIES


def build_bias(ref, place):
    ref["table"][...] = jnp.zeros((HEADS, 1024), F32)
    ref["table"][:, :961] = (16.0 * LOG2E) * jax.nn.sigmoid(ref["tab"][...])
    high = ref["table"][...].astype(BF16).astype(F32)
    low = ref["table"][...] - high
    k = lax.broadcasted_iota(jnp.int32, (HEAD, 1024), 1)
    b = lax.broadcasted_iota(jnp.int32, (HEAD, 1024), 0)
    chosen = jnp.where((k - 31 * ((k * 2115) >> 16)) == 30 - b, 1.0, 0.0)
    k, lane = iotas((1024, 512))
    spread = onehot(((k * 2115) >> 16) == (lane >> 4))
    terms = None
    for part in (high, low):
        left = (part[:, None, :] * chosen[None]).reshape(HEADS * HEAD, 1024).astype(BF16)
        term = mm(left, spread)
        terms = term if terms is None else terms + term
    lane = lax.broadcasted_iota(jnp.int32, (HEAD, 512), 1)
    shift = 15 - (lane & 15)
    q, p = iotas((TOK, TOK))
    last_row = place.r == 3
    last_col = place.c == 63
    row_cut = jnp.where((q >> 7) != (p >> 7), jnp.where(last_row, 0.0, 1.0), 1.0)
    col_cut = jnp.where(((q >> 3) & 1) != ((p >> 3) & 1), jnp.where(last_col, 0.0, 1.0), 1.0)
    allowed = row_cut * col_cut
    for h in range(HEADS):
        rows = terms[h * HEAD : (h + 1) * HEAD, :]
        for bit in range(4):
            moved = pltpu.roll(rows, HEAD - (1 << bit), 0)
            rows = jnp.where(((shift >> bit) & 1) == 1, moved, rows)
        rows = jnp.exp2(rows[:16])
        for turn in range(8):
            turned = rows if turn == 0 else pltpu.roll(rows, 512 - 16 * turn, 1)
            for whole in range(2):
                row = 15 - (whole * 8 + turn)
                at = slice(row * 16, (row + 1) * 16)
                ref["bias"][h, at, :] = turned[:, whole * 128 : whole * 128 + 256] * allowed[at, :]


def copy_out(*refs):
    count = len(refs) // 2
    for index in range(count):
        refs[count + index][...] = refs[index][...]


def hand_over(arrays):
    vmem = pl.BlockSpec(memory_space=pltpu.VMEM)
    return pl.pallas_call(
        copy_out,
        name="results",
        out_shape=tuple(jax.ShapeDtypeStruct(a.shape, a.dtype) for a in arrays),
        in_specs=[vmem] * len(arrays),
        out_specs=(vmem,) * len(arrays),
    )(*arrays)


def per_device(
    image,
    w_qkv,
    b_qkv,
    logit_scale,
    bias_table,
    w_proj,
    b_proj,
    gain_attn,
    shift_attn,
    w_merge,
    gain_merge,
    shift_merge,
    grad_out,
):
    vmem = pl.BlockSpec(memory_space=pltpu.VMEM)
    smem = pl.BlockSpec(memory_space=pltpu.SMEM)
    anywhere = pl.BlockSpec(memory_space=pl.ANY)
    factor = 1.0 / math.sqrt(16384)
    outs = pl.pallas_call(
        functools.partial(kernel, factor),
        name="block",
        out_shape=(
            jax.ShapeDtypeStruct((MTOK, WIDE), BF16),
            jax.ShapeDtypeStruct((TOK, CH), BF16),
            jax.ShapeDtypeStruct((24, 128), F32),
            jax.ShapeDtypeStruct((8, 128), F32),
            jax.ShapeDtypeStruct((64, 128), F32),
        ),
        in_specs=[anywhere] * 5 + [vmem, smem] + [vmem] * 6,
        out_specs=(vmem,) * 5,
        scratch_shapes=[pltpu.VMEM(shape, dtype) for shape, dtype in SCRATCH.values()]
        + [
            pltpu.SemaphoreType.DMA((COPIES,)),
            pltpu.SemaphoreType.DMA((COPIES,)),
            pltpu.SemaphoreType.DMA((len(LOADS),)),
        ],
        compiler_params=pltpu.CompilerParams(
            collective_id=0, has_side_effects=True, vmem_limit_bytes=60 * 2**20
        ),
    )(
        image.reshape(TOK, CH),
        grad_out.reshape(MTOK, WIDE),
        w_qkv,
        w_proj,
        w_merge,
        b_qkv,
        logit_scale,
        bias_table,
        b_proj.reshape(1, -1),
        gain_attn.reshape(1, -1),
        shift_attn.reshape(1, -1),
        gain_merge.reshape(1, -1),
        shift_merge.reshape(1, -1),
    )
    merged, gimage, gqkv, gproj, gmerge = hand_over(outs)
    return (
        merged.reshape(8, 8, WIDE),
        gimage.reshape(16, 16, CH),
        gqkv.reshape(-1),
        gproj.reshape(-1),
        gmerge.reshape(-1),
    )


def solution(mesh):
    whole = P()
    tiles = P("rows", "cols", None)
    flat = P(("cols", "rows"))
    return jax.shard_map(
        per_device,
        mesh=mesh,
        in_specs=(tiles,) + (whole,) * 11 + (tiles,),
        out_specs=(tiles, tiles, flat, flat, flat),
        check_vma=False,
    )
```

```python
import functools
import math

import jax
import jax.numpy as jnp
from jax import lax
from jax.experimental import pallas as pl
from jax.experimental.pallas import tpu as pltpu
from jax.sharding import PartitionSpec as P

MESH = pl.DeviceIdType.MESH
F32 = jnp.float32
BF16 = jnp.bfloat16

CH = 512
HEADS = 16
HEAD = 32
TOK = 256
MTOK = 64
WIDE = 1024
EPS_NORM = 1e-05
EPS_COS = 1e-06
LOG2E = math.log2(math.e)
LN2 = math.log(2.0)

NN = (((1,), (0,)), ((), ()))
NT = (((1,), (1,)), ((), ()))
TN = (((0,), (0,)), ((), ()))


def mm(left, right, dims=NN):
    return lax.dot_general(left, right, dims, preferred_element_type=F32)


def iotas(shape):
    return (
        lax.broadcasted_iota(jnp.int32, shape, 0),
        lax.broadcasted_iota(jnp.int32, shape, 1),
    )


def onehot(cond):
    return jnp.where(cond, 1.0, 0.0).astype(BF16)


def quad_source(t):
    quad, a, b = t >> 6, (t >> 3) & 7, t & 7
    return ((quad >> 1) * 8 + a) * 16 + (quad & 1) * 8 + b


def group_source(t):
    member, quad, i, j = t >> 6, (t >> 4) & 3, (t >> 2) & 3, t & 3
    row = (quad >> 1) * 8 + 2 * i + (member & 1)
    col = (quad & 1) * 8 + 2 * j + (member >> 1)
    return row * 16 + col


def merged_source(u):
    quad, i, j = u >> 4, (u >> 2) & 3, u & 3
    return ((quad >> 1) * 4 + i) * 8 + (quad & 1) * 4 + j


def channel_source(t):
    core, parity = t >> 8, (t >> 7) & 1
    x, y, z = (t >> 5) & 3, (t >> 3) & 3, t & 7
    owner = (x >> 1) * 128 + z * 16 + y * 4 + (x & 1) * 2 + core
    return 2 * owner + parity


class Place:
    def __init__(self):
        self.c = lax.axis_index("cols")
        self.r = lax.axis_index("rows")
        self.x = (self.c // 32) * 2 + self.r // 2
        self.z = (self.c // 4) % 8
        self.y = self.c % 4
        self.k = self.r % 2
        self.coord = {"x": self.x, "y": self.y, "z": self.z}

    def beside(self, dc, dr):
        return ((self.c + dc + 64) % 64, (self.r + dr + 4) % 4)

    def sibling(self):
        return (self.c, self.r + 1 - 2 * self.k)

    def along(self, axis, step, core=None):
        core = self.k if core is None else core
        at = dict(self.coord)
        size = AXES[axis]
        at[axis] = (at[axis] + step + size) % size
        return ((at["x"] // 2) * 32 + at["z"] * 4 + at["y"], (at["x"] % 2) * 2 + core)


OPERANDS = (
    "image", "gout", "wq_in", "wp_in", "wm_in", "bq", "ls", "tab", "bp", "ga", "sa", "gm", "sm"
)
LOADS = (("image", "tile"), ("gout", "gtile"), ("wq_in", "wq"), ("wp_in", "wp"), ("wm_in", "wm"))
RESULTS = ("merged", "gimage", "gqkv", "gproj", "gmerge")
AXES = {"x": 4, "y": 4, "z": 8}
ORDERS = (("x", "y"), ("y", "x"))

SCRATCH = {
    "wq": ((CH, 3 * CH), BF16),
    "wp": ((CH, CH), BF16),
    "wm": ((4 * CH, WIDE), BF16),
    "wqT": ((3 * CH, CH), BF16),
    "wpT": ((CH, CH), BF16),
    "sentX": ((4, 64, CH), BF16),
    "gotX": ((4, 64, CH), BF16),
    "sentG": ((4, 16, WIDE), BF16),
    "gotG": ((4, 16, WIDE), BF16),
    "sentO": ((4, 16, WIDE), BF16),
    "gotO": ((4, 16, WIDE), BF16),
    "sentI": ((4, 64, CH), BF16),
    "gotI": ((4, 64, CH), BF16),
    "table": ((HEADS, 1024), F32),
    "bias": ((HEADS, TOK, TOK), F32),
    "colq": ((3 * CH, 128), F32),
    "colp": ((CH, 128), F32),
    "colg": ((CH, 128), F32),
    "cols": ((CH, 128), F32),
    "xT": ((CH, TOK), BF16),
    "qs": ((CH, TOK), BF16),
    "qu": ((CH, TOK), F32),
    "ku": ((CH, TOK), F32),
    "kb": ((CH, TOK), BF16),
    "vb": ((CH, TOK), BF16),
    "qinv": ((HEADS, TOK), F32),
    "kinv": ((HEADS, TOK), F32),
    "linv": ((HEADS, TOK), F32),
    "soft": ((HEADS, TOK, TOK), BF16),
    "att": ((CH, TOK), BF16),
    "normed": ((CH, TOK), F32),
    "dA": ((CH, TOK), BF16),
    "upT": ((CH, TOK), F32),
    "rows": ((2, TOK, TOK), BF16),
    "rowsGot": ((TOK, TOK), BF16),
    "attP": ((2, TOK, TOK), BF16),
    "attGot": ((TOK, TOK), BF16),
    "dproj": ((CH, TOK), BF16),
    "dprojGot": ((CH, TOK), BF16),
    "dmix": ((2, 3 * TOK, TOK), BF16),
    "dmixGot": ((2, 3 * TOK, TOK), BF16),
    "tile": ((TOK, CH), BF16),
    "gtile": ((MTOK, WIDE), BF16),
    "gath": ((4, 2, MTOK, 256), BF16),
    "gathAll": ((8, MTOK, 256), BF16),
    "dredAll": ((2, 8, MTOK, CH), BF16),
    "ms1a": ((8, 4, 16, 256), BF16),
    "mr1a": ((7, 4, 16, 256), BF16),
    "ms2a": ((4, 16, 256), BF16),
    "mr2a": ((3, 16, 256), BF16),
    "ms1b": ((4, 8, 16, 256), BF16),
    "mr1b": ((3, 8, 16, 256), BF16),
    "ms2b": ((8, 16, 256), BF16),
    "mr2b": ((7, 16, 256), BF16),
    "qs1": ((2, 2, 4, 4, 4, 16, 128), BF16),
    "qr1": ((2, 2, 3, 4, 4, 16, 128), BF16),
    "qs2": ((2, 2, 4, 4, 16, 128), BF16),
    "qr2": ((2, 2, 3, 4, 16, 128), BF16),
    "qs3": ((2, 8, 16, 128), BF16),
    "qr3": ((2, 7, 16, 128), BF16),
    "fold0": ((128 * 16, 128), F32),
    "fold1": ((128 * 16, 128), F32),
}
COPIES = 96


def kernel(factor, *refs):
    names = OPERANDS + RESULTS + tuple(SCRATCH) + ("ssem", "rsem", "lsem")
    ref = dict(zip(names, refs, strict=True))
    place = Place()
    used = [0]
    pending = []

    def send(src, dst, device):
        index = used[0]
        used[0] += 1
        copy = pltpu.make_async_remote_copy(
            src_ref=src,
            dst_ref=dst,
            send_sem=ref["ssem"].at[index],
            recv_sem=ref["rsem"].at[index],
            device_id=device,
            device_id_type=MESH,
        )
        copy.start()
        pending.append(copy)
        return copy

    partners = [(dc, dr) for dc in (-1, 0, 1) for dr in (-1, 0, 1) if dc * dr >= 0 and (dc, dr) != (0, 0)]
    greeted = [place.beside(dc, dr) for dc, dr in partners] + [place.sibling()]
    for axis, size in AXES.items():
        greeted += [place.along(axis, step) for step in range(1, size)]
    greeted += [place.along("x", step, 1 - place.k) for step in range(1, 4)]
    barrier = pltpu.get_barrier_semaphore()
    for device in greeted:
        pl.semaphore_signal(barrier, inc=1, device_id=device, device_id_type=MESH)

    loads = {}
    for index, (src, dst) in enumerate(LOADS):
        loads[dst] = pltpu.make_async_copy(ref[src], ref[dst], ref["lsem"].at[index])
        loads[dst].start()

    t, n = iotas((TOK, TOK))
    to_quads = onehot(n == quad_source(t))
    from_quads = onehot(t == quad_source(n))
    groups = onehot(n == group_source(t))
    u, v = iotas((MTOK, MTOK))
    merged_quads = onehot(v == merged_source(u))
    merged_back = onehot(u == merged_source(v))
    loads["tile"].wait()
    ref["sentX"][...] = mm(to_quads, ref["tile"][...]).astype(BF16).reshape(4, 64, CH)
    loads["gtile"].wait()
    ref["sentG"][...] = mm(merged_quads, ref["gtile"][...]).astype(BF16).reshape(4, 16, WIDE)
    pl.semaphore_wait(barrier, len(greeted))

    def to_window(sent, got):
        copies = []
        for quad in (2, 1, 0):
            rh, ch = quad >> 1, quad & 1
            copies.append(
                send(ref[sent].at[quad], ref[got].at[3 - quad], place.beside(ch - 1, rh - 1))
            )
        ref[got][0] = ref[sent][3]
        return copies

    def to_image(sent, got):
        copies = []
        for quad in (3, 2, 1):
            qr, qc = quad >> 1, quad & 1
            copies.append(send(ref[sent].at[quad], ref[got].at[3 - quad], place.beside(qc, qr)))
        ref[got][3] = ref[sent][0]
        return copies

    came_x = to_window("sentX", "gotX")
    came_g = to_window("sentG", "gotG")

    def column(src, dst, size):
        ref[dst][...] = jnp.broadcast_to(ref[src][...].reshape(1, size), (128, size)).T

    column("bq", "colq", 3 * CH)
    column("bp", "colp", CH)
    column("ga", "colg", CH)
    column("sa", "cols", CH)

    def wide(name, rows=slice(None)):
        col = ref[name][rows, :]
        return jnp.concatenate([col, col], axis=1)

    build_bias(ref, place)
    loads["wq"].wait()
    loads["wp"].wait()
    for part in range(3):
        ref["wqT"][part * CH : (part + 1) * CH, :] = ref["wq"][:, part * CH : (part + 1) * CH].T
    ref["wpT"][...] = ref["wp"][...].T

    for copy in came_x:
        copy.wait_recv()
    x = mm(from_quads, ref["gotX"][...].reshape(TOK, CH)).astype(BF16)
    q = mm(ref["wqT"][:CH, :], x, NT) + wide("colq", slice(0, CH))
    k = mm(ref["wqT"][CH : 2 * CH, :], x, NT) + wide("colq", slice(CH, 2 * CH))
    val = mm(ref["wqT"][2 * CH :, :], x, NT) + wide("colq", slice(2 * CH, 3 * CH))
    ref["vb"][...] = val.astype(BF16)
    q = q.reshape(HEADS, HEAD, TOK)
    k = k.reshape(HEADS, HEAD, TOK)
    qinv = lax.rsqrt(jnp.sum(q * q, axis=1, keepdims=True) + EPS_COS)
    kinv = lax.rsqrt(jnp.sum(k * k, axis=1, keepdims=True) + EPS_COS)
    qu = (q * qinv).reshape(CH, TOK)
    ku = (k * kinv).reshape(CH, TOK)
    ref["qinv"][...] = qinv.reshape(HEADS, TOK)
    ref["kinv"][...] = kinv.reshape(HEADS, TOK)
    ref["qu"][...] = qu
    ref["ku"][...] = ku
    ref["kb"][...] = ku.astype(BF16)

    def scale_of(h):
        return jnp.exp(jnp.full((1, TOK), ref["ls"][h], F32))

    for h in range(HEADS):
        at = slice(h * HEAD, (h + 1) * HEAD)
        ref["qs"][at, :] = (qu[at, :] * (scale_of(h) * LOG2E)).astype(BF16)
    ref["xT"][...] = x.astype(F32).T.astype(BF16)

    a, b = iotas((CH, CH))
    owners = onehot(b == channel_source(a))
    ref["rows"][...] = mm(owners, x, NT).astype(BF16).reshape(2, TOK, TOK)
    came_rows = send(ref["rows"].at[1 - place.k], ref["rowsGot"], place.sibling())

    def attend(h):
        at = pl.ds(pl.multiple_of(h * HEAD, HEAD), HEAD)
        raised = jnp.exp2(mm(ref["kb"][at, :], ref["qs"][at, :], TN)) * ref["bias"][h]
        total = jnp.sum(raised, axis=0, keepdims=True)
        low = raised.astype(BF16)
        ref["soft"][h] = low
        inverse = 1.0 / total
        ref["linv"][pl.ds(h, 1), :] = inverse
        ref["att"][at, :] = (mm(ref["vb"][at, :], low) * inverse).astype(BF16)

    for h in range(HEADS):
        attend(h)

    att = ref["att"][...]
    projected = mm(ref["wpT"][...], att) + wide("colp")
    average = jnp.mean(projected, axis=0, keepdims=True)
    centered = projected - average
    inverse = lax.rsqrt(jnp.mean(centered * centered, axis=0, keepdims=True) + EPS_NORM)
    normed = centered * inverse
    ref["normed"][...] = normed
    gain = wide("colg")
    branch = ref["xT"][...].astype(F32) + normed * gain + wide("cols")
    result = branch.astype(BF16)

    blocks = branch.reshape(16, 4, 8, TOK)
    ordered = jnp.concatenate([blocks[:, owner].reshape(128, TOK) for owner in range(4)], axis=0)
    ordered = ordered.astype(BF16)
    for member in range(4):
        pick = groups[member * 64 : (member + 1) * 64, :]
        part = mm(pick, ordered, NT).astype(BF16)
        lanes = slice((member & 1) * 128, (member & 1) * 128 + 128)
        for owner in range(4):
            x, core = (member >> 1) * 2 + (owner >> 1), owner & 1
            ref["gath"][x, core, :, lanes] = part[:, owner * 128 : (owner + 1) * 128]
    came_tokens = []
    ref["gathAll"][place.k] = ref["gath"][place.x, place.k]
    for step in (2, 1, 3, 0):
        for other in range(2):
            if step or other:
                core = place.k + other - 2 * other * place.k
                x = (place.x + step) % 4
                device = place.along("x", step, core)
                slot = 2 * step + place.k
                came_tokens.append(send(ref["gath"].at[x, core], ref["gathAll"].at[slot], device))
    loads["wm"].wait()
    reduced = None
    for member in range(4):
        pick = groups[member * 64 : (member + 1) * 64, :]
        gathered = mm(pick, result, NT).astype(BF16)
        term = mm(gathered, ref["wm"][member * CH : (member + 1) * CH, :])
        reduced = term if reduced is None else reduced + term
    m_average = jnp.mean(reduced, axis=-1, keepdims=True)
    m_centered = reduced - m_average
    m_inverse = lax.rsqrt(jnp.mean(m_centered * m_centered, axis=-1, keepdims=True) + EPS_NORM)
    m_normed = m_centered * m_inverse
    merged = m_normed * ref["gm"][...] + ref["sm"][...]
    ref["sentO"][...] = merged.astype(BF16).reshape(4, 16, WIDE)
    for copy in came_g:
        copy.wait_recv()
    came_o = to_image("sentO", "gotO")
    scaled = ref["gotG"][...].reshape(MTOK, WIDE).astype(F32) * ref["gm"][...]
    m_mean = jnp.mean(scaled, axis=-1, keepdims=True)
    m_proj = jnp.mean(scaled * m_normed, axis=-1, keepdims=True)
    d_reduced = (m_inverse * (scaled - m_mean - m_normed * m_proj)).astype(BF16)
    came_dred = {}
    came_half = [[], []]
    for part in range(2):
        ref["dredAll"][part, place.k] = d_reduced[:, part * CH : (part + 1) * CH]
        own = ref["dredAll"].at[part, place.k]
        for step in (2, 1, 3):
            slot = ref["dredAll"].at[part, 2 * step + place.k]
            came_dred[part, step] = send(own, slot, place.along("x", step))
        came_half[part].append(send(own, own, place.sibling()))

    def pass_on(part):
        for step in (1, 3, 2):
            came_dred[part, step].wait_recv()
            slot = ref["dredAll"].at[part, 2 * step + place.k]
            came_half[part].append(send(slot, slot, place.sibling()))

    def merge_grads(part):
        if part == 0:
            for copy in came_tokens:
                copy.wait_recv()
        for copy in came_half[part]:
            copy.wait_recv()
        tokens = ref["gathAll"][...].reshape(8 * MTOK, 256)
        grads = mm(tokens, ref["dredAll"][part].reshape(8 * MTOK, CH), TN).reshape(8, 4, 8, CH)
        shares = jnp.concatenate([grads[..., :256], grads[..., 256:]], axis=2).astype(BF16)
        if part == 0:
            ref["ms1a"][...] = shares
        else:
            for y in range(4):
                ref["ms1b"][y] = shares[:, y]
        return start_stage(*m_refs(part, 0))

    d_in = [
        mm(d_reduced, ref["wm"][member * CH : (member + 1) * CH, :], NT).astype(BF16)
        for member in range(4)
    ]
    upstream = mm(jnp.concatenate(d_in, axis=0), groups, TN)
    ref["upT"][...] = upstream
    a_scaled = upstream * gain
    a_mean = jnp.mean(a_scaled, axis=0, keepdims=True)
    a_proj = jnp.mean(a_scaled * normed, axis=0, keepdims=True)
    ref["dproj"][...] = (inverse * (a_scaled - a_mean - normed * a_proj)).astype(BF16)
    came_dproj = send(ref["dproj"], ref["dprojGot"], place.sibling())
    ref["attP"][...] = mm(owners, att).astype(BF16).reshape(2, TOK, TOK)
    came_att = send(ref["attP"].at[1 - place.k], ref["attGot"], place.sibling())

    def start_stage(src, dst, axis):
        mine, size = place.coord[axis], AXES[axis]
        copies = []
        for step in range(1, size):
            slot = dst.at[step - 1]
            copies.append(send(src.at[(mine + step) % size], slot, place.along(axis, step)))
        return copies

    def end_stage(src, dst, axis, copies):
        total = src[place.coord[axis]].astype(F32)
        for step, copy in enumerate(copies):
            copy.wait_recv()
            total = total + dst[step].astype(F32)
        return total

    def q_refs(half, zh, stage):
        if stage == 2:
            return ref["qs3"].at[half], ref["qr3"].at[half]
        number = str(stage + 1)
        return ref["qs" + number].at[half, zh], ref["qr" + number].at[half, zh]

    def start_q(half, stage):
        if stage == 2:
            return [start_stage(*q_refs(half, 0, 2), "z")]
        return [start_stage(*q_refs(half, zh, stage), ORDERS[zh][stage]) for zh in range(2)]

    def end_q(half, stage):
        for zh in range(2):
            total = end_stage(*q_refs(half, zh, stage), ORDERS[zh][stage], q_stage[half][zh])
            if stage == 0:
                ref["qs2"][half, zh] = total.astype(BF16)
            else:
                ref["qs3"][half, 4 * zh : 4 * zh + 4] = total.astype(BF16)

    q_stage = []
    m_copies = []

    def m_refs(part, stage):
        name = str(stage + 1) + "ab"[part]
        return ref["ms" + name], ref["mr" + name], "zy"[part ^ stage]

    def second_m(part):
        total = end_stage(*m_refs(part, 0), m_copies[part])
        ref["ms2" + "ab"[part]][...] = total.astype(BF16)
        m_copies[part] = start_stage(*m_refs(part, 1))

    d_attended = mm(ref["wp"][...], ref["dproj"][...]).astype(BF16)
    ref["dA"][...] = d_attended

    def attend_back(h):
        at = pl.ds(pl.multiple_of(h * HEAD, HEAD), HEAD)
        linv = ref["linv"][pl.ds(h, 1), :]
        d_att = ref["dA"][at, :].astype(F32) * linv
        delta = jnp.sum(d_att * ref["att"][at, :].astype(F32), axis=0, keepdims=True)
        d_low = d_att.astype(BF16)
        soft = ref["soft"][h]
        d_soft = mm(ref["vb"][at, :], d_low, TN)
        d_scores = (soft.astype(F32) * (d_soft - delta)).astype(BF16)
        scale = scale_of(h)
        d_value = mm(d_low, soft, NT)
        d_qu = mm(ref["kb"][at, :], d_scores) * scale
        d_ku = mm(ref["qs"][at, :], d_scores, NT) * LN2
        q_unit, k_unit = ref["qu"][at, :], ref["ku"][at, :]
        d_q = ref["qinv"][pl.ds(h, 1), :] * (
            d_qu - q_unit * jnp.sum(q_unit * d_qu, axis=0, keepdims=True)
        )
        d_k = ref["kinv"][pl.ds(h, 1), :] * (
            d_ku - k_unit * jnp.sum(k_unit * d_ku, axis=0, keepdims=True)
        )
        for part, values in enumerate((d_q, d_k, d_value)):
            rows = pl.ds(pl.multiple_of(part * 256 + (h & 7) * HEAD, HEAD), HEAD)
            ref["dmix"][h >> 3, rows, :] = values.astype(BF16)

    folds = (ref["fold0"], ref["fold1"])

    def put(half, unit, values):
        for lane in range(2):
            part = values[:, lane * 128 : (lane + 1) * 128]
            folds[half][pl.ds(unit + lane, 128, stride=16), :] = part

    came_mix = []

    def send_mix(half):
        came_mix.append(send(ref["dmix"].at[half], ref["dmixGot"].at[half], place.sibling()))

    def q_grads(half):
        came_mix[half].wait_recv()
        own_rows = ref["rows"][place.k]
        for part in range(3):
            cols = slice(part * 256, (part + 1) * 256)
            values = mm(own_rows, ref["dmix"][half, cols, :], NT)
            values = values + mm(ref["rowsGot"][...], ref["dmixGot"][half, cols, :], NT)
            put(half, 2 * part, values[:128])
            put(half, 6 + 2 * part, values[128:])
        for first in range(4):
            for second in range(4):
                at = pl.ds((first * 4 + second) * 128, 128)
                share = folds[half][at, :].astype(BF16).reshape(8, 16, 128)
                ref["qs1"][half, 0, first, second] = share[:4]
                ref["qs1"][half, 1, second, first] = share[4:]
        q_stage.append(start_q(half, 0))

    for h in range(8):
        attend_back(h)
    send_mix(0)
    came_rows.wait_recv()
    came_att.wait_recv()
    came_dproj.wait_recv()
    own_att = ref["attP"][place.k]
    for piece in range(2):
        cols = slice(piece * 256, (piece + 1) * 256)
        part = mm(own_att, ref["dproj"][cols, :], NT)
        part = part + mm(ref["attGot"][...], ref["dprojGot"][cols, :], NT)
        put(0, 12 + 2 * piece, part[:128])
        put(1, 12 + 2 * piece, part[128:])
    for h in range(8, 12):
        attend_back(h)
    q_grads(0)
    pass_on(0)
    for h in range(12, 16):
        attend_back(h)
    send_mix(1)
    m_copies.append(merge_grads(0))
    q_grads(1)
    pass_on(1)
    end_q(0, 0)
    q_stage[0] = start_q(0, 1)

    d_rows = None
    for block in range(6):
        cols = slice((block % 3) * 512 + (block // 3) * 256, (block % 3) * 512 + (block // 3) * 256 + 256)
        rows = slice((block % 3) * 256, (block % 3) * 256 + 256)
        term = mm(ref["wq"][:, cols], ref["dmix"][block // 3, rows, :])
        d_rows = term if d_rows is None else d_rows + term
    d_image = (ref["upT"][...] + d_rows).astype(BF16)
    ref["sentI"][...] = mm(to_quads, d_image, NT).astype(BF16).reshape(4, 64, CH)
    came_i = to_image("sentI", "gotI")
    m_copies.append(merge_grads(1))

    end_q(0, 1)
    q_stage[0] = start_q(0, 2)
    end_q(1, 0)
    q_stage[1] = start_q(1, 1)
    second_m(1)
    second_m(0)

    for copy in came_o:
        copy.wait_recv()
    ref["merged"][...] = mm(merged_back, ref["gotO"][...].reshape(MTOK, WIDE)).astype(BF16)

    end_q(1, 1)
    q_stage[1] = start_q(1, 2)

    for copy in came_i:
        copy.wait_recv()
    ref["gimage"][...] = mm(from_quads, ref["gotI"][...].reshape(TOK, CH)).astype(BF16)

    for half in range(2):
        total = end_stage(*q_refs(half, 0, 2), "z", q_stage[half][0]) * factor
        for parity in range(2):
            for part in range(3):
                row, unit = parity * 12 + part * 4 + half * 2, parity * 6 + part * 2
                ref["gqkv"][row : row + 2, :] = total[unit : unit + 2]
        ref["gproj"][half * 4 : half * 4 + 4, :] = total[12:]
    for half in range(2):
        total = end_stage(*m_refs(half, 1), m_copies[half]) * factor
        for fold in range(2):
            for lane in range(2):
                part = total[fold * 8 : fold * 8 + 8, lane * 128 : (lane + 1) * 128]
                ref["gmerge"][pl.ds(half * 4 + fold * 2 + lane, 8, stride=8), :] = part
    for copy in pending:
        copy.wait_send()
    assert used[0] <= COPIES


def build_bias(ref, place):
    ref["table"][...] = jnp.zeros((HEADS, 1024), F32)
    ref["table"][:, :961] = (16.0 * LOG2E) * jax.nn.sigmoid(ref["tab"][...])
    high = ref["table"][...].astype(BF16).astype(F32)
    low = ref["table"][...] - high
    k = lax.broadcasted_iota(jnp.int32, (HEAD, 1024), 1)
    b = lax.broadcasted_iota(jnp.int32, (HEAD, 1024), 0)
    chosen = jnp.where((k - 31 * ((k * 2115) >> 16)) == 30 - b, 1.0, 0.0)
    k, lane = iotas((1024, 512))
    spread = onehot(((k * 2115) >> 16) == (lane >> 4))
    terms = None
    for part in (high, low):
        left = (part[:, None, :] * chosen[None]).reshape(HEADS * HEAD, 1024).astype(BF16)
        term = mm(left, spread)
        terms = term if terms is None else terms + term
    lane = lax.broadcasted_iota(jnp.int32, (HEAD, 512), 1)
    shift = 15 - (lane & 15)
    q, p = iotas((TOK, TOK))
    last_row = place.r == 3
    last_col = place.c == 63
    row_cut = jnp.where((q >> 7) != (p >> 7), jnp.where(last_row, 0.0, 1.0), 1.0)
    col_cut = jnp.where(((q >> 3) & 1) != ((p >> 3) & 1), jnp.where(last_col, 0.0, 1.0), 1.0)
    allowed = row_cut * col_cut
    for h in range(HEADS):
        rows = terms[h * HEAD : (h + 1) * HEAD, :]
        for bit in range(4):
            moved = pltpu.roll(rows, HEAD - (1 << bit), 0)
            rows = jnp.where(((shift >> bit) & 1) == 1, moved, rows)
        rows = jnp.exp2(rows[:16])
        for turn in range(8):
            turned = rows if turn == 0 else pltpu.roll(rows, 512 - 16 * turn, 1)
            for whole in range(2):
                row = 15 - (whole * 8 + turn)
                at = slice(row * 16, (row + 1) * 16)
                ref["bias"][h, at, :] = turned[:, whole * 128 : whole * 128 + 256] * allowed[at, :]


def copy_out(*refs):
    count = len(refs) // 2
    for index in range(count):
        refs[count + index][...] = refs[index][...]


def hand_over(arrays):
    vmem = pl.BlockSpec(memory_space=pltpu.VMEM)
    return pl.pallas_call(
        copy_out,
        name="results",
        out_shape=tuple(jax.ShapeDtypeStruct(a.shape, a.dtype) for a in arrays),
        in_specs=[vmem] * len(arrays),
        out_specs=(vmem,) * len(arrays),
    )(*arrays)


def per_device(
    image,
    w_qkv,
    b_qkv,
    logit_scale,
    bias_table,
    w_proj,
    b_proj,
    gain_attn,
    shift_attn,
    w_merge,
    gain_merge,
    shift_merge,
    grad_out,
):
    vmem = pl.BlockSpec(memory_space=pltpu.VMEM)
    smem = pl.BlockSpec(memory_space=pltpu.SMEM)
    anywhere = pl.BlockSpec(memory_space=pl.ANY)
    factor = 1.0 / math.sqrt(16384)
    outs = pl.pallas_call(
        functools.partial(kernel, factor),
        name="block",
        out_shape=(
            jax.ShapeDtypeStruct((MTOK, WIDE), BF16),
            jax.ShapeDtypeStruct((TOK, CH), BF16),
            jax.ShapeDtypeStruct((24, 128), F32),
            jax.ShapeDtypeStruct((8, 128), F32),
            jax.ShapeDtypeStruct((64, 128), F32),
        ),
        in_specs=[anywhere] * 5 + [vmem, smem] + [vmem] * 6,
        out_specs=(vmem,) * 5,
        scratch_shapes=[pltpu.VMEM(shape, dtype) for shape, dtype in SCRATCH.values()]
        + [
            pltpu.SemaphoreType.DMA((COPIES,)),
            pltpu.SemaphoreType.DMA((COPIES,)),
            pltpu.SemaphoreType.DMA((len(LOADS),)),
        ],
        compiler_params=pltpu.CompilerParams(
            collective_id=0, has_side_effects=True, vmem_limit_bytes=60 * 2**20
        ),
    )(
        image.reshape(TOK, CH),
        grad_out.reshape(MTOK, WIDE),
        w_qkv,
        w_proj,
        w_merge,
        b_qkv,
        logit_scale,
        bias_table,
        b_proj.reshape(1, -1),
        gain_attn.reshape(1, -1),
        shift_attn.reshape(1, -1),
        gain_merge.reshape(1, -1),
        shift_merge.reshape(1, -1),
    )
    merged, gimage, gqkv, gproj, gmerge = hand_over(outs)
    return (
        merged.reshape(8, 8, WIDE),
        gimage.reshape(16, 16, CH),
        gqkv.reshape(-1),
        gproj.reshape(-1),
        gmerge.reshape(-1),
    )


def solution(mesh):
    whole = P()
    tiles = P("rows", "cols", None)
    flat = P(("cols", "rows"))
    return jax.shard_map(
        per_device,
        mesh=mesh,
        in_specs=(tiles,) + (whole,) * 11 + (tiles,),
        out_specs=(tiles, tiles, flat, flat, flat),
        check_vma=False,
    )
```

```python
import functools
import math

import jax
import jax.numpy as jnp
from jax import lax
from jax.experimental import pallas as pl
from jax.experimental.pallas import tpu as pltpu
from jax.sharding import PartitionSpec as P

MESH = pl.DeviceIdType.MESH
F32 = jnp.float32
BF16 = jnp.bfloat16

CH = 512
HEADS = 16
HEAD = 32
TOK = 256
MTOK = 64
WIDE = 1024
EPS_NORM = 1e-05
EPS_COS = 1e-06
LOG2E = math.log2(math.e)
LN2 = math.log(2.0)

NN = (((1,), (0,)), ((), ()))
NT = (((1,), (1,)), ((), ()))
TN = (((0,), (0,)), ((), ()))


def mm(left, right, dims=NN):
    return lax.dot_general(left, right, dims, preferred_element_type=F32)


def iotas(shape):
    return (
        lax.broadcasted_iota(jnp.int32, shape, 0),
        lax.broadcasted_iota(jnp.int32, shape, 1),
    )


def onehot(cond):
    return jnp.where(cond, 1.0, 0.0).astype(BF16)


def quad_source(t):
    quad, a, b = t >> 6, (t >> 3) & 7, t & 7
    return ((quad >> 1) * 8 + a) * 16 + (quad & 1) * 8 + b


def group_source(t):
    member, quad, i, j = t >> 6, (t >> 4) & 3, (t >> 2) & 3, t & 3
    row = (quad >> 1) * 8 + 2 * i + (member & 1)
    col = (quad & 1) * 8 + 2 * j + (member >> 1)
    return row * 16 + col


def merged_source(u):
    quad, i, j = u >> 4, (u >> 2) & 3, u & 3
    return ((quad >> 1) * 4 + i) * 8 + (quad & 1) * 4 + j


def channel_source(t):
    core, parity = t >> 8, (t >> 7) & 1
    x, y, z = (t >> 5) & 3, (t >> 3) & 3, t & 7
    owner = (x >> 1) * 128 + z * 16 + y * 4 + (x & 1) * 2 + core
    return 2 * owner + parity


class Place:
    def __init__(self):
        self.c = lax.axis_index("cols")
        self.r = lax.axis_index("rows")
        self.x = (self.c // 32) * 2 + self.r // 2
        self.z = (self.c // 4) % 8
        self.y = self.c % 4
        self.k = self.r % 2
        self.coord = {"x": self.x, "y": self.y, "z": self.z}

    def beside(self, dc, dr):
        return ((self.c + dc + 64) % 64, (self.r + dr + 4) % 4)

    def sibling(self):
        return (self.c, self.r + 1 - 2 * self.k)

    def along(self, axis, step, core=None):
        core = self.k if core is None else core
        at = dict(self.coord)
        size = AXES[axis]
        at[axis] = (at[axis] + step + size) % size
        return ((at["x"] // 2) * 32 + at["z"] * 4 + at["y"], (at["x"] % 2) * 2 + core)


OPERANDS = (
    "image", "gout", "wq_in", "wp_in", "wm_in", "bq", "ls", "tab", "bp", "ga", "sa", "gm", "sm"
)
LOADS = (("image", "tile"), ("gout", "gtile"), ("wq_in", "wq"), ("wp_in", "wp"), ("wm_in", "wm"))
RESULTS = ("merged", "gimage", "gqkv", "gproj", "gmerge")
AXES = {"x": 4, "y": 4, "z": 8}
ORDERS = (("x", "y"), ("y", "x"))

SCRATCH = {
    "wq": ((CH, 3 * CH), BF16),
    "wp": ((CH, CH), BF16),
    "wm": ((4 * CH, WIDE), BF16),
    "wqT": ((3 * CH, CH), BF16),
    "wpT": ((CH, CH), BF16),
    "sentX": ((4, 64, CH), BF16),
    "gotX": ((4, 64, CH), BF16),
    "sentG": ((4, 16, WIDE), BF16),
    "gotG": ((4, 16, WIDE), BF16),
    "sentO": ((4, 16, WIDE), BF16),
    "gotO": ((4, 16, WIDE), BF16),
    "sentI": ((4, 64, CH), BF16),
    "gotI": ((4, 64, CH), BF16),
    "table": ((HEADS, 1024), F32),
    "bias": ((HEADS, TOK, TOK), F32),
    "colq": ((3 * CH, 128), F32),
    "colp": ((CH, 128), F32),
    "colg": ((CH, 128), F32),
    "cols": ((CH, 128), F32),
    "xT": ((CH, TOK), BF16),
    "qs": ((CH, TOK), BF16),
    "qu": ((CH, TOK), F32),
    "ku": ((CH, TOK), F32),
    "kb": ((CH, TOK), BF16),
    "vb": ((CH, TOK), BF16),
    "qinv": ((HEADS, TOK), F32),
    "kinv": ((HEADS, TOK), F32),
    "linv": ((HEADS, TOK), F32),
    "soft": ((HEADS, TOK, TOK), BF16),
    "att": ((CH, TOK), BF16),
    "normed": ((CH, TOK), F32),
    "dA": ((CH, TOK), BF16),
    "upT": ((CH, TOK), F32),
    "rows": ((2, TOK, TOK), BF16),
    "rowsGot": ((TOK, TOK), BF16),
    "attP": ((2, TOK, TOK), BF16),
    "attGot": ((TOK, TOK), BF16),
    "dproj": ((CH, TOK), BF16),
    "dprojGot": ((CH, TOK), BF16),
    "dmix": ((2, 3 * TOK, TOK), BF16),
    "dmixGot": ((2, 3 * TOK, TOK), BF16),
    "tile": ((TOK, CH), BF16),
    "gtile": ((MTOK, WIDE), BF16),
    "gath": ((4, 2, MTOK, 256), BF16),
    "gathAll": ((8, MTOK, 256), BF16),
    "dredAll": ((2, 8, MTOK, CH), BF16),
    "ms1a": ((8, 4, 16, 256), BF16),
    "mr1a": ((7, 4, 16, 256), BF16),
    "ms2a": ((4, 16, 256), BF16),
    "mr2a": ((3, 16, 256), BF16),
    "ms1b": ((4, 8, 16, 256), BF16),
    "mr1b": ((3, 8, 16, 256), BF16),
    "ms2b": ((8, 16, 256), BF16),
    "mr2b": ((7, 16, 256), BF16),
    "qs1": ((2, 2, 4, 4, 4, 16, 128), BF16),
    "qr1": ((2, 2, 3, 4, 4, 16, 128), BF16),
    "qs2": ((2, 2, 4, 4, 16, 128), BF16),
    "qr2": ((2, 2, 3, 4, 16, 128), BF16),
    "qs3": ((2, 8, 16, 128), BF16),
    "qr3": ((2, 7, 16, 128), BF16),
    "fold0": ((128 * 16, 128), F32),
    "fold1": ((128 * 16, 128), F32),
}
COPIES = 96


def kernel(factor, *refs):
    names = OPERANDS + RESULTS + tuple(SCRATCH) + ("ssem", "rsem", "lsem")
    ref = dict(zip(names, refs, strict=True))
    place = Place()
    used = [0]
    pending = []

    def send(src, dst, device):
        index = used[0]
        used[0] += 1
        copy = pltpu.make_async_remote_copy(
            src_ref=src,
            dst_ref=dst,
            send_sem=ref["ssem"].at[index],
            recv_sem=ref["rsem"].at[index],
            device_id=device,
            device_id_type=MESH,
        )
        copy.start()
        pending.append(copy)
        return copy

    partners = [(dc, dr) for dc in (-1, 0, 1) for dr in (-1, 0, 1) if dc * dr >= 0 and (dc, dr) != (0, 0)]
    greeted = [place.beside(dc, dr) for dc, dr in partners] + [place.sibling()]
    for axis, size in AXES.items():
        greeted += [place.along(axis, step) for step in range(1, size)]
    greeted += [place.along("x", step, 1 - place.k) for step in range(1, 4)]
    loads = {}
    for index, (src, dst) in enumerate(LOADS):
        loads[dst] = pltpu.make_async_copy(ref[src], ref[dst], ref["lsem"].at[index])
        loads[dst].start()

    barrier = pltpu.get_barrier_semaphore()
    for device in greeted:
        pl.semaphore_signal(barrier, inc=1, device_id=device, device_id_type=MESH)

    t, n = iotas((TOK, TOK))
    to_quads = onehot(n == quad_source(t))
    from_quads = onehot(t == quad_source(n))
    groups = onehot(n == group_source(t))
    u, v = iotas((MTOK, MTOK))
    merged_quads = onehot(v == merged_source(u))
    merged_back = onehot(u == merged_source(v))
    loads["tile"].wait()
    ref["sentX"][...] = mm(to_quads, ref["tile"][...]).astype(BF16).reshape(4, 64, CH)
    loads["gtile"].wait()
    ref["sentG"][...] = mm(merged_quads, ref["gtile"][...]).astype(BF16).reshape(4, 16, WIDE)
    pl.semaphore_wait(barrier, len(greeted))

    def to_window(sent, got):
        copies = []
        for quad in (2, 1, 0):
            rh, ch = quad >> 1, quad & 1
            copies.append(
                send(ref[sent].at[quad], ref[got].at[3 - quad], place.beside(ch - 1, rh - 1))
            )
        ref[got][0] = ref[sent][3]
        return copies

    def to_image(sent, got):
        copies = []
        for quad in (3, 2, 1):
            qr, qc = quad >> 1, quad & 1
            copies.append(send(ref[sent].at[quad], ref[got].at[3 - quad], place.beside(qc, qr)))
        ref[got][3] = ref[sent][0]
        return copies

    came_x = to_window("sentX", "gotX")
    came_g = to_window("sentG", "gotG")

    def column(src, dst, size):
        ref[dst][...] = jnp.broadcast_to(ref[src][...].reshape(1, size), (128, size)).T

    column("bq", "colq", 3 * CH)
    column("bp", "colp", CH)
    column("ga", "colg", CH)
    column("sa", "cols", CH)

    def wide(name, rows=slice(None)):
        col = ref[name][rows, :]
        return jnp.concatenate([col, col], axis=1)

    build_bias(ref, place)
    loads["wq"].wait()
    loads["wp"].wait()
    for part in range(3):
        ref["wqT"][part * CH : (part + 1) * CH, :] = ref["wq"][:, part * CH : (part + 1) * CH].T
    ref["wpT"][...] = ref["wp"][...].T

    for copy in came_x:
        copy.wait_recv()
    x = mm(from_quads, ref["gotX"][...].reshape(TOK, CH)).astype(BF16)
    q = mm(ref["wqT"][:CH, :], x, NT) + wide("colq", slice(0, CH))
    k = mm(ref["wqT"][CH : 2 * CH, :], x, NT) + wide("colq", slice(CH, 2 * CH))
    val = mm(ref["wqT"][2 * CH :, :], x, NT) + wide("colq", slice(2 * CH, 3 * CH))
    ref["vb"][...] = val.astype(BF16)
    q = q.reshape(HEADS, HEAD, TOK)
    k = k.reshape(HEADS, HEAD, TOK)
    qinv = lax.rsqrt(jnp.sum(q * q, axis=1, keepdims=True) + EPS_COS)
    kinv = lax.rsqrt(jnp.sum(k * k, axis=1, keepdims=True) + EPS_COS)
    qu = (q * qinv).reshape(CH, TOK)
    ku = (k * kinv).reshape(CH, TOK)
    ref["qinv"][...] = qinv.reshape(HEADS, TOK)
    ref["kinv"][...] = kinv.reshape(HEADS, TOK)
    ref["qu"][...] = qu
    ref["ku"][...] = ku
    ref["kb"][...] = ku.astype(BF16)

    def scale_of(h):
        return jnp.exp(jnp.full((1, TOK), ref["ls"][h], F32))

    for h in range(HEADS):
        at = slice(h * HEAD, (h + 1) * HEAD)
        ref["qs"][at, :] = (qu[at, :] * (scale_of(h) * LOG2E)).astype(BF16)
    ref["xT"][...] = x.astype(F32).T.astype(BF16)

    a, b = iotas((CH, CH))
    owners = onehot(b == channel_source(a))
    ref["rows"][...] = mm(owners, x, NT).astype(BF16).reshape(2, TOK, TOK)
    came_rows = send(ref["rows"].at[1 - place.k], ref["rowsGot"], place.sibling())

    def attend(h):
        at = pl.ds(pl.multiple_of(h * HEAD, HEAD), HEAD)
        raised = jnp.exp2(mm(ref["kb"][at, :], ref["qs"][at, :], TN)) * ref["bias"][h]
        total = jnp.sum(raised, axis=0, keepdims=True)
        low = raised.astype(BF16)
        ref["soft"][h] = low
        inverse = 1.0 / total
        ref["linv"][pl.ds(h, 1), :] = inverse
        ref["att"][at, :] = (mm(ref["vb"][at, :], low) * inverse).astype(BF16)

    for h in range(HEADS):
        attend(h)

    att = ref["att"][...]
    projected = mm(ref["wpT"][...], att) + wide("colp")
    average = jnp.mean(projected, axis=0, keepdims=True)
    centered = projected - average
    inverse = lax.rsqrt(jnp.mean(centered * centered, axis=0, keepdims=True) + EPS_NORM)
    normed = centered * inverse
    ref["normed"][...] = normed
    gain = wide("colg")
    branch = ref["xT"][...].astype(F32) + normed * gain + wide("cols")
    result = branch.astype(BF16)

    blocks = branch.reshape(16, 4, 8, TOK)
    ordered = jnp.concatenate([blocks[:, owner].reshape(128, TOK) for owner in range(4)], axis=0)
    ordered = ordered.astype(BF16)
    for member in range(4):
        pick = groups[member * 64 : (member + 1) * 64, :]
        part = mm(pick, ordered, NT).astype(BF16)
        lanes = slice((member & 1) * 128, (member & 1) * 128 + 128)
        for owner in range(4):
            x, core = (member >> 1) * 2 + (owner >> 1), owner & 1
            ref["gath"][x, core, :, lanes] = part[:, owner * 128 : (owner + 1) * 128]
    came_tokens = []
    ref["gathAll"][place.k] = ref["gath"][place.x, place.k]
    for step in (2, 1, 3, 0):
        for other in range(2):
            if step or other:
                core = place.k + other - 2 * other * place.k
                x = (place.x + step) % 4
                device = place.along("x", step, core)
                slot = 2 * step + place.k
                came_tokens.append(send(ref["gath"].at[x, core], ref["gathAll"].at[slot], device))
    loads["wm"].wait()
    reduced = None
    for member in range(4):
        pick = groups[member * 64 : (member + 1) * 64, :]
        gathered = mm(pick, result, NT).astype(BF16)
        term = mm(gathered, ref["wm"][member * CH : (member + 1) * CH, :])
        reduced = term if reduced is None else reduced + term
    m_average = jnp.mean(reduced, axis=-1, keepdims=True)
    m_centered = reduced - m_average
    m_inverse = lax.rsqrt(jnp.mean(m_centered * m_centered, axis=-1, keepdims=True) + EPS_NORM)
    m_normed = m_centered * m_inverse
    merged = m_normed * ref["gm"][...] + ref["sm"][...]
    ref["sentO"][...] = merged.astype(BF16).reshape(4, 16, WIDE)
    for copy in came_g:
        copy.wait_recv()
    came_o = to_image("sentO", "gotO")
    scaled = ref["gotG"][...].reshape(MTOK, WIDE).astype(F32) * ref["gm"][...]
    m_mean = jnp.mean(scaled, axis=-1, keepdims=True)
    m_proj = jnp.mean(scaled * m_normed, axis=-1, keepdims=True)
    d_reduced = (m_inverse * (scaled - m_mean - m_normed * m_proj)).astype(BF16)
    came_dred = {}
    came_half = [[], []]
    for part in range(2):
        ref["dredAll"][part, place.k] = d_reduced[:, part * CH : (part + 1) * CH]
        own = ref["dredAll"].at[part, place.k]
        for step in (2, 1, 3):
            slot = ref["dredAll"].at[part, 2 * step + place.k]
            came_dred[part, step] = send(own, slot, place.along("x", step))
        came_half[part].append(send(own, own, place.sibling()))

    def pass_on(part):
        for step in (1, 3, 2):
            came_dred[part, step].wait_recv()
            slot = ref["dredAll"].at[part, 2 * step + place.k]
            came_half[part].append(send(slot, slot, place.sibling()))

    def merge_grads(part):
        if part == 0:
            for copy in came_tokens:
                copy.wait_recv()
        for copy in came_half[part]:
            copy.wait_recv()
        tokens = ref["gathAll"][...].reshape(8 * MTOK, 256)
        grads = mm(tokens, ref["dredAll"][part].reshape(8 * MTOK, CH), TN).reshape(8, 4, 8, CH)
        shares = jnp.concatenate([grads[..., :256], grads[..., 256:]], axis=2).astype(BF16)
        if part == 0:
            ref["ms1a"][...] = shares
        else:
            for y in range(4):
                ref["ms1b"][y] = shares[:, y]
        return start_stage(*m_refs(part, 0))

    d_in = [
        mm(d_reduced, ref["wm"][member * CH : (member + 1) * CH, :], NT).astype(BF16)
        for member in range(4)
    ]
    upstream = mm(jnp.concatenate(d_in, axis=0), groups, TN)
    ref["upT"][...] = upstream
    a_scaled = upstream * gain
    a_mean = jnp.mean(a_scaled, axis=0, keepdims=True)
    a_proj = jnp.mean(a_scaled * normed, axis=0, keepdims=True)
    ref["dproj"][...] = (inverse * (a_scaled - a_mean - normed * a_proj)).astype(BF16)
    came_dproj = send(ref["dproj"], ref["dprojGot"], place.sibling())
    ref["attP"][...] = mm(owners, att).astype(BF16).reshape(2, TOK, TOK)
    came_att = send(ref["attP"].at[1 - place.k], ref["attGot"], place.sibling())

    def start_stage(src, dst, axis):
        mine, size = place.coord[axis], AXES[axis]
        copies = []
        for step in range(1, size):
            slot = dst.at[step - 1]
            copies.append(send(src.at[(mine + step) % size], slot, place.along(axis, step)))
        return copies

    def end_stage(src, dst, axis, copies):
        total = src[place.coord[axis]].astype(F32)
        for step, copy in enumerate(copies):
            copy.wait_recv()
            total = total + dst[step].astype(F32)
        return total

    def q_refs(half, zh, stage):
        if stage == 2:
            return ref["qs3"].at[half], ref["qr3"].at[half]
        number = str(stage + 1)
        return ref["qs" + number].at[half, zh], ref["qr" + number].at[half, zh]

    def start_q(half, stage):
        if stage == 2:
            return [start_stage(*q_refs(half, 0, 2), "z")]
        return [start_stage(*q_refs(half, zh, stage), ORDERS[zh][stage]) for zh in range(2)]

    def end_q(half, stage):
        for zh in range(2):
            total = end_stage(*q_refs(half, zh, stage), ORDERS[zh][stage], q_stage[half][zh])
            if stage == 0:
                ref["qs2"][half, zh] = total.astype(BF16)
            else:
                ref["qs3"][half, 4 * zh : 4 * zh + 4] = total.astype(BF16)

    q_stage = []
    m_copies = []

    def m_refs(part, stage):
        name = str(stage + 1) + "ab"[part]
        return ref["ms" + name], ref["mr" + name], "zy"[part ^ stage]

    def second_m(part):
        total = end_stage(*m_refs(part, 0), m_copies[part])
        ref["ms2" + "ab"[part]][...] = total.astype(BF16)
        m_copies[part] = start_stage(*m_refs(part, 1))

    d_attended = mm(ref["wp"][...], ref["dproj"][...]).astype(BF16)
    ref["dA"][...] = d_attended

    def attend_back(h):
        at = pl.ds(pl.multiple_of(h * HEAD, HEAD), HEAD)
        linv = ref["linv"][pl.ds(h, 1), :]
        d_att = ref["dA"][at, :].astype(F32) * linv
        delta = jnp.sum(d_att * ref["att"][at, :].astype(F32), axis=0, keepdims=True)
        d_low = d_att.astype(BF16)
        soft = ref["soft"][h]
        d_soft = mm(ref["vb"][at, :], d_low, TN)
        d_scores = (soft.astype(F32) * (d_soft - delta)).astype(BF16)
        scale = scale_of(h)
        d_value = mm(d_low, soft, NT)
        d_qu = mm(ref["kb"][at, :], d_scores) * scale
        d_ku = mm(ref["qs"][at, :], d_scores, NT) * LN2
        q_unit, k_unit = ref["qu"][at, :], ref["ku"][at, :]
        d_q = ref["qinv"][pl.ds(h, 1), :] * (
            d_qu - q_unit * jnp.sum(q_unit * d_qu, axis=0, keepdims=True)
        )
        d_k = ref["kinv"][pl.ds(h, 1), :] * (
            d_ku - k_unit * jnp.sum(k_unit * d_ku, axis=0, keepdims=True)
        )
        for part, values in enumerate((d_q, d_k, d_value)):
            rows = pl.ds(pl.multiple_of(part * 256 + (h & 7) * HEAD, HEAD), HEAD)
            ref["dmix"][h >> 3, rows, :] = values.astype(BF16)

    folds = (ref["fold0"], ref["fold1"])

    def put(half, unit, values):
        for lane in range(2):
            part = values[:, lane * 128 : (lane + 1) * 128]
            folds[half][pl.ds(unit + lane, 128, stride=16), :] = part

    came_mix = []

    def send_mix(half):
        came_mix.append(send(ref["dmix"].at[half], ref["dmixGot"].at[half], place.sibling()))

    def q_grads(half):
        own_rows = ref["rows"][place.k]
        spans = [slice(part * 256, (part + 1) * 256) for part in range(3)]
        own = [mm(own_rows, ref["dmix"][half, cols, :], NT) for cols in spans]
        came_mix[half].wait_recv()
        for part, cols in enumerate(spans):
            values = own[part] + mm(ref["rowsGot"][...], ref["dmixGot"][half, cols, :], NT)
            put(half, 2 * part, values[:128])
            put(half, 6 + 2 * part, values[128:])
        for first in range(4):
            for second in range(4):
                at = pl.ds((first * 4 + second) * 128, 128)
                share = folds[half][at, :].astype(BF16).reshape(8, 16, 128)
                ref["qs1"][half, 0, first, second] = share[:4]
                ref["qs1"][half, 1, second, first] = share[4:]
        q_stage.append(start_q(half, 0))

    for h in range(8):
        attend_back(h)
    send_mix(0)
    came_rows.wait_recv()
    came_att.wait_recv()
    came_dproj.wait_recv()
    own_att = ref["attP"][place.k]
    for piece in range(2):
        cols = slice(piece * 256, (piece + 1) * 256)
        part = mm(own_att, ref["dproj"][cols, :], NT)
        part = part + mm(ref["attGot"][...], ref["dprojGot"][cols, :], NT)
        put(0, 12 + 2 * piece, part[:128])
        put(1, 12 + 2 * piece, part[128:])
    for h in range(8, 12):
        attend_back(h)
    q_grads(0)
    pass_on(0)
    for h in range(12, 16):
        attend_back(h)
    send_mix(1)
    m_copies.append(merge_grads(0))
    q_grads(1)
    pass_on(1)
    end_q(0, 0)
    q_stage[0] = start_q(0, 1)

    d_rows = None
    for block in range(6):
        cols = slice((block % 3) * 512 + (block // 3) * 256, (block % 3) * 512 + (block // 3) * 256 + 256)
        rows = slice((block % 3) * 256, (block % 3) * 256 + 256)
        term = mm(ref["wq"][:, cols], ref["dmix"][block // 3, rows, :])
        d_rows = term if d_rows is None else d_rows + term
    d_image = (ref["upT"][...] + d_rows).astype(BF16)
    ref["sentI"][...] = mm(to_quads, d_image, NT).astype(BF16).reshape(4, 64, CH)
    came_i = to_image("sentI", "gotI")
    m_copies.append(merge_grads(1))

    end_q(0, 1)
    q_stage[0] = start_q(0, 2)
    end_q(1, 0)
    q_stage[1] = start_q(1, 1)
    second_m(1)
    second_m(0)

    for copy in came_o:
        copy.wait_recv()
    ref["merged"][...] = mm(merged_back, ref["gotO"][...].reshape(MTOK, WIDE)).astype(BF16)

    end_q(1, 1)
    q_stage[1] = start_q(1, 2)

    for copy in came_i:
        copy.wait_recv()
    ref["gimage"][...] = mm(from_quads, ref["gotI"][...].reshape(TOK, CH)).astype(BF16)

    for half in range(2):
        total = end_stage(*q_refs(half, 0, 2), "z", q_stage[half][0]) * factor
        for parity in range(2):
            for part in range(3):
                row, unit = parity * 12 + part * 4 + half * 2, parity * 6 + part * 2
                ref["gqkv"][row : row + 2, :] = total[unit : unit + 2]
        ref["gproj"][half * 4 : half * 4 + 4, :] = total[12:]
    for half in range(2):
        total = end_stage(*m_refs(half, 1), m_copies[half]) * factor
        for fold in range(2):
            for lane in range(2):
                part = total[fold * 8 : fold * 8 + 8, lane * 128 : (lane + 1) * 128]
                ref["gmerge"][pl.ds(half * 4 + fold * 2 + lane, 8, stride=8), :] = part
    for copy in pending:
        copy.wait_send()
    assert used[0] <= COPIES


def build_bias(ref, place):
    ref["table"][...] = jnp.zeros((HEADS, 1024), F32)
    ref["table"][:, :961] = (16.0 * LOG2E) * jax.nn.sigmoid(ref["tab"][...])
    high = ref["table"][...].astype(BF16).astype(F32)
    low = ref["table"][...] - high
    k = lax.broadcasted_iota(jnp.int32, (HEAD, 1024), 1)
    b = lax.broadcasted_iota(jnp.int32, (HEAD, 1024), 0)
    chosen = jnp.where((k - 31 * ((k * 2115) >> 16)) == 30 - b, 1.0, 0.0)
    k, lane = iotas((1024, 512))
    spread = onehot(((k * 2115) >> 16) == (lane >> 4))
    terms = None
    for part in (high, low):
        left = (part[:, None, :] * chosen[None]).reshape(HEADS * HEAD, 1024).astype(BF16)
        term = mm(left, spread)
        terms = term if terms is None else terms + term
    lane = lax.broadcasted_iota(jnp.int32, (HEAD, 512), 1)
    shift = 15 - (lane & 15)
    q, p = iotas((TOK, TOK))
    last_row = place.r == 3
    last_col = place.c == 63
    row_cut = jnp.where((q >> 7) != (p >> 7), jnp.where(last_row, 0.0, 1.0), 1.0)
    col_cut = jnp.where(((q >> 3) & 1) != ((p >> 3) & 1), jnp.where(last_col, 0.0, 1.0), 1.0)
    allowed = row_cut * col_cut
    for h in range(HEADS):
        rows = terms[h * HEAD : (h + 1) * HEAD, :]
        for bit in range(4):
            moved = pltpu.roll(rows, HEAD - (1 << bit), 0)
            rows = jnp.where(((shift >> bit) & 1) == 1, moved, rows)
        rows = jnp.exp2(rows[:16])
        for turn in range(8):
            turned = rows if turn == 0 else pltpu.roll(rows, 512 - 16 * turn, 1)
            for whole in range(2):
                row = 15 - (whole * 8 + turn)
                at = slice(row * 16, (row + 1) * 16)
                ref["bias"][h, at, :] = turned[:, whole * 128 : whole * 128 + 256] * allowed[at, :]


def copy_out(*refs):
    count = len(refs) // 2
    for index in range(count):
        refs[count + index][...] = refs[index][...]


def hand_over(arrays):
    vmem = pl.BlockSpec(memory_space=pltpu.VMEM)
    return pl.pallas_call(
        copy_out,
        name="results",
        out_shape=tuple(jax.ShapeDtypeStruct(a.shape, a.dtype) for a in arrays),
        in_specs=[vmem] * len(arrays),
        out_specs=(vmem,) * len(arrays),
    )(*arrays)


def per_device(
    image,
    w_qkv,
    b_qkv,
    logit_scale,
    bias_table,
    w_proj,
    b_proj,
    gain_attn,
    shift_attn,
    w_merge,
    gain_merge,
    shift_merge,
    grad_out,
):
    vmem = pl.BlockSpec(memory_space=pltpu.VMEM)
    smem = pl.BlockSpec(memory_space=pltpu.SMEM)
    anywhere = pl.BlockSpec(memory_space=pl.ANY)
    factor = 1.0 / math.sqrt(16384)
    outs = pl.pallas_call(
        functools.partial(kernel, factor),
        name="block",
        out_shape=(
            jax.ShapeDtypeStruct((MTOK, WIDE), BF16),
            jax.ShapeDtypeStruct((TOK, CH), BF16),
            jax.ShapeDtypeStruct((24, 128), F32),
            jax.ShapeDtypeStruct((8, 128), F32),
            jax.ShapeDtypeStruct((64, 128), F32),
        ),
        in_specs=[anywhere] * 5 + [vmem, smem] + [vmem] * 6,
        out_specs=(vmem,) * 5,
        scratch_shapes=[pltpu.VMEM(shape, dtype) for shape, dtype in SCRATCH.values()]
        + [
            pltpu.SemaphoreType.DMA((COPIES,)),
            pltpu.SemaphoreType.DMA((COPIES,)),
            pltpu.SemaphoreType.DMA((len(LOADS),)),
        ],
        compiler_params=pltpu.CompilerParams(
            collective_id=0, has_side_effects=True, vmem_limit_bytes=60 * 2**20
        ),
    )(
        image.reshape(TOK, CH),
        grad_out.reshape(MTOK, WIDE),
        w_qkv,
        w_proj,
        w_merge,
        b_qkv,
        logit_scale,
        bias_table,
        b_proj.reshape(1, -1),
        gain_attn.reshape(1, -1),
        shift_attn.reshape(1, -1),
        gain_merge.reshape(1, -1),
        shift_merge.reshape(1, -1),
    )
    merged, gimage, gqkv, gproj, gmerge = hand_over(outs)
    return (
        merged.reshape(8, 8, WIDE),
        gimage.reshape(16, 16, CH),
        gqkv.reshape(-1),
        gproj.reshape(-1),
        gmerge.reshape(-1),
    )


def solution(mesh):
    whole = P()
    tiles = P("rows", "cols", None)
    flat = P(("cols", "rows"))
    return jax.shard_map(
        per_device,
        mesh=mesh,
        in_specs=(tiles,) + (whole,) * 11 + (tiles,),
        out_specs=(tiles, tiles, flat, flat, flat),
        check_vma=False,
    )
```
